256 devices in a mesh: inst: 32 (over z_lo, y, x), tp: 8 (over z_hi, core).
Axes of the slice: x: 4, y: 4, z: 8 (z_hi: 4, z_lo: 2; z = z_hi * 2 + z_lo), core: 2. Of those that a mesh axis runs over, the one named last changes fastest.
Arguments:
- kv_cache: bfloat16 [256, 2048, 2048], P('inst', None, 'tp'), may hold values from -8 to 8
- queries: bfloat16 [384, 6, 8192], P('inst', None, 'tp'), may hold values from -8 to 8
- fresh_kv: bfloat16 [384, 6, 2048], P('inst', None, 'tp'), may hold values from -6 to 6
- out_proj: bfloat16 [8192, 4096], P('tp'), may hold values from -0.0625 to 0.0625
- moving: int32 [128], replicated, may hold values from 0 to 255, as said below
- destination: int32 [128], replicated, may hold values from 0 to 31, as said below
- round_pages: int32 [128, 3], replicated, may hold values from 0 to 8, as said below
- lengths: int32 [256], replicated, may hold values from 1 to 2042, as said below
Outputs:
- attended: bfloat16 [384, 6, 4096], P('inst', None, 'tp')
- arrived_cache: bfloat16 [128, 2048, 2048], P('inst', None, 'tp')
The draws below stay inside these ranges and needn't reach their ends.
Inputs may be any that keep to these rules, and one draw needn't show every extreme that they name: `moving`: each instance sends 4 distinct rows of its own. (destination[m] - moving[m] // 8) mod 32 is 1, 2, 8 or 16; every instance sends one row at each of these distances and receives one from each. round_pages[m, 0] >= 1, and a row's counts sum to ceil(lengths[moving[m]] / 128); some row sends 8 pages in one round. `lengths`: migrating rows are longer than 1792; some migrating row has the largest length.
All inputs are finite; a program needn't handle non-finite values.
Results may differ from the reference program's by a relative error of at most 0.0057.
Values may be sent and summed in bfloat16 or wider, within the bound.
A program may use at most 128 MiB of HBM per device.

```python
import jax
import jax.numpy as jnp
from jax import lax

HEADS = 64
KV_HEADS = 8
HEAD_DIM = 128
OUT_COLS = 4096
PAGE = 128
R_DEV = 8
CACHE_LEN = 2048
ROUNDS = 3
ROUND_STEPS = 2
ARRIVAL_SLOTS = 4
STEPS = 6
SLOTS = 12
INSTANCES = 32
ROWS = 256
MIGRANTS = 128
PG_CAP = 8


def draw_plan(key):
    plan_key = jax.random.fold_in(key, 700)
    keys_list = jax.random.split(plan_key, 8)
    distances = jnp.array([1, 2, INSTANCES // 4, INSTANCES // 2], jnp.int32)
    inst_ids = jnp.arange(INSTANCES, dtype=jnp.int32)
    row_ids = jnp.arange(R_DEV, dtype=jnp.int32)
    rank_keys = jax.random.randint(keys_list[0], (INSTANCES, R_DEV), 0, 1 << 20) * R_DEV + row_ids[None, :]
    ordering = jnp.argsort(rank_keys, axis=1)[:, :ARRIVAL_SLOTS].astype(jnp.int32)
    moving = (inst_ids[:, None] * R_DEV + ordering).reshape(MIGRANTS).astype(jnp.int32)
    lane_ids = jnp.arange(ARRIVAL_SLOTS, dtype=jnp.int32)
    lane_keys = jax.random.randint(keys_list[4], (INSTANCES, ARRIVAL_SLOTS), 0, 1 << 20) * ARRIVAL_SLOTS + lane_ids[None, :]
    lane_order = jnp.argsort(lane_keys, axis=1).astype(jnp.int32)
    picked_distance = jnp.take(distances, lane_order)
    destination = ((inst_ids[:, None] + picked_distance) % INSTANCES).reshape(MIGRANTS).astype(jnp.int32)
    lengths = jax.random.randint(keys_list[1], (ROWS,), 1, CACHE_LEN - STEPS + 1)
    migrant_lengths = jax.random.randint(keys_list[2], (MIGRANTS,), CACHE_LEN - 2 * PAGE + 1, CACHE_LEN - STEPS + 1)
    longest = jax.random.randint(keys_list[3], (), 0, MIGRANTS)
    migrant_lengths = jnp.where(jnp.arange(MIGRANTS) == longest, CACHE_LEN - STEPS, migrant_lengths)
    lengths = lengths.at[moving].set(migrant_lengths).astype(jnp.int32)
    page_total = (migrant_lengths + PAGE - 1) // PAGE
    first_round = jax.random.randint(keys_list[6], (MIGRANTS,), jnp.maximum(1, page_total - 2 * PG_CAP), jnp.minimum(PG_CAP, page_total) + 1)
    first_round = jnp.where(jnp.arange(MIGRANTS) == longest, jnp.minimum(PG_CAP, page_total), first_round)
    remaining = page_total - first_round
    second_round = jax.random.randint(keys_list[7], (MIGRANTS,), jnp.maximum(0, remaining - PG_CAP), jnp.minimum(PG_CAP, remaining) + 1)
    third_round = remaining - second_round
    round_pages = jnp.stack([first_round, second_round, third_round], axis=1).astype(jnp.int32)
    return (moving, destination, round_pages, lengths)


def draw_moving(key, part):
    plan_values = draw_plan(key)
    return plan_values[0]


def draw_destination(key, part):
    plan_values = draw_plan(key)
    return plan_values[1]


def draw_round_pages(key, part):
    plan_values = draw_plan(key)
    return plan_values[2]


def draw_lengths(key, part):
    plan_values = draw_plan(key)
    return plan_values[3]


def draw_kv_cache(key, part):
    key = jax.random.fold_in(key, 11)
    first_key = jax.random.fold_in(key, 0)
    shape = (ROWS, CACHE_LEN, KV_HEADS, 2, HEAD_DIM)
    values = jnp.clip(jax.random.normal(first_key, shape, jnp.float32), -6.0, 6.0)
    return values.reshape(ROWS, CACHE_LEN, KV_HEADS * 2 * HEAD_DIM).astype(jnp.bfloat16)


def draw_queries(key, part):
    key = jax.random.fold_in(key, 12)
    first_key = jax.random.fold_in(key, 0)
    shape = (INSTANCES * SLOTS, STEPS, HEADS, HEAD_DIM)
    values = jnp.clip(jax.random.normal(first_key, shape, jnp.float32), -6.0, 6.0)
    return values.reshape(INSTANCES * SLOTS, STEPS, HEADS * HEAD_DIM).astype(jnp.bfloat16)


def levels(rng, extent, cuts, smallest, top_value):
    gain = 1.0
    for position, blocks in cuts:
        steps = jax.random.uniform(jax.random.fold_in(jax.random.fold_in(rng, 6), position), (blocks,), jnp.float32, smallest / len(cuts), top_value / len(cuts))
        gain = gain * jnp.repeat(jnp.exp(steps), extent[position] // blocks).reshape((-1,) + (1,) * (len(extent) - 1 - position))
    return gain


def bell_draw(stream_key, shape, width, most, pieces=(), kind=jnp.bfloat16):
    entries = width * jax.random.normal(stream_key, shape, jnp.float32)
    if pieces:
        entries = entries * levels(stream_key, shape, pieces, -0.22, 0.18)
    return jnp.clip(entries, -most, most).astype(kind)


def setup_inputs(seed: int = 0) -> dict:
    splits = jax.random.split(jax.random.key(seed), 9)
    kv_cache = draw_kv_cache(jax.random.fold_in(splits[8], 71), 0)
    queries = draw_queries(jax.random.fold_in(splits[8], 71), 0)
    fresh_kv = bell_draw(splits[2], (INSTANCES * SLOTS, STEPS, KV_HEADS * 2 * HEAD_DIM), 1.0, 6.0, ((0, 32), (2, 8)))
    out_proj = bell_draw(splits[3], (HEADS * HEAD_DIM, OUT_COLS), (HEADS * HEAD_DIM) ** -0.5, 0.0625, ((0, 8),))
    moving = draw_moving(jax.random.fold_in(splits[8], 71), 0)
    destination = draw_destination(jax.random.fold_in(splits[8], 71), 0)
    round_pages = draw_round_pages(jax.random.fold_in(splits[8], 71), 0)
    lengths = draw_lengths(jax.random.fold_in(splits[8], 71), 0)
    return dict(kv_cache=kv_cache, queries=queries, fresh_kv=fresh_kv, out_proj=out_proj, moving=moving, destination=destination, round_pages=round_pages, lengths=lengths)


minus_large = -1.0e30


def plan_tables(moving, destination, round_pages, lengths):
    source_inst = (moving // R_DEV).astype(jnp.int32)
    distance = (destination - source_inst) % INSTANCES
    distances = jnp.array([1, 2, INSTANCES // 4, INSTANCES // 2], jnp.int32)
    lane_index = jnp.sum(jnp.where(distance[:, None] == distances[None, :], jnp.arange(4, dtype=jnp.int32)[None, :], 0), axis=1).astype(jnp.int32)
    done_round = jnp.max(jnp.where(round_pages > 0, jnp.arange(ROUNDS, dtype=jnp.int32)[None, :], 0), axis=1).astype(jnp.int32)
    base_length = jnp.take(lengths, moving.astype(jnp.int32)).astype(jnp.int32)
    return source_inst, lane_index, done_round, base_length


def attend_slot(kv_cache, row_index, length, active_steps, query_rows, fresh_rows):
    group_size = HEADS // KV_HEADS
    row_block = lax.dynamic_index_in_dim(kv_cache, row_index, 0, keepdims=False)
    stored = row_block.reshape(CACHE_LEN, KV_HEADS, 2, HEAD_DIM).astype(jnp.float32)
    fresh_all = fresh_rows.reshape(STEPS, KV_HEADS, 2, HEAD_DIM).astype(jnp.float32)
    query_heads = query_rows.reshape(STEPS, KV_HEADS, group_size, HEAD_DIM).astype(jnp.float32)
    score_scale = HEAD_DIM ** -0.5
    cache_scores = jnp.einsum("tkgd,lkd->tkgl", query_heads, stored[:, :, 0]) * score_scale
    fresh_scores = jnp.einsum("tkgd,ukd->tkgu", query_heads, fresh_all[:, :, 0]) * score_scale
    cache_ok = jnp.arange(CACHE_LEN, dtype=jnp.int32) < length
    step_ids = jnp.arange(STEPS, dtype=jnp.int32)
    fresh_ok = (step_ids[None, :] <= step_ids[:, None]) & active_steps[None, :]
    cache_scores = jnp.where(cache_ok[None, None, None, :], cache_scores, minus_large)
    fresh_scores = jnp.where(fresh_ok[:, None, None, :], fresh_scores, minus_large)
    top_score = jnp.maximum(jnp.max(cache_scores, axis=-1), jnp.max(fresh_scores, axis=-1))
    cache_exp = jnp.exp(cache_scores - top_score[..., None])
    fresh_exp = jnp.exp(fresh_scores - top_score[..., None])
    denominator = jnp.sum(cache_exp, axis=-1) + jnp.sum(fresh_exp, axis=-1)
    cache_weight = (cache_exp / denominator[..., None]).astype(jnp.bfloat16)
    fresh_weight = (fresh_exp / denominator[..., None]).astype(jnp.bfloat16)
    mixed_values = jnp.einsum("tkgl,lkd->tkgd", cache_weight.astype(jnp.float32), stored[:, :, 1])
    mixed_values = mixed_values + jnp.einsum("tkgu,ukd->tkgd", fresh_weight.astype(jnp.float32), fresh_all[:, :, 1])
    return mixed_values.reshape(STEPS, HEADS * HEAD_DIM).astype(jnp.bfloat16)


def land_slot(kv_cache, row_index, length, active_steps, fresh_rows):
    row_block = lax.dynamic_index_in_dim(kv_cache, row_index, 0, keepdims=False)
    positions = jnp.arange(CACHE_LEN, dtype=jnp.int32)
    kept_rows = jnp.where((positions < length)[:, None], row_block, jnp.zeros((), row_block.dtype))
    order_index = (jnp.cumsum(active_steps.astype(jnp.int32)) - 1).astype(jnp.int32)
    for step_index in range(STEPS):
        target = length + order_index[step_index]
        hit_row = (positions == target) & active_steps[step_index]
        kept_rows = jnp.where(hit_row[:, None], fresh_rows[step_index][None, :], kept_rows)
    return kept_rows


def reference(kv_cache, queries, fresh_kv, out_proj, moving, destination, round_pages, lengths):
    source_inst, lane_index, done_round, base_length = plan_tables(moving, destination, round_pages, lengths)
    slot_ids = jnp.arange(INSTANCES * SLOTS, dtype=jnp.int32)
    owner_inst = slot_ids // SLOTS
    within = slot_ids % SLOTS
    is_home = within < R_DEV
    home_row = (owner_inst * R_DEV + jnp.minimum(within, R_DEV - 1)).astype(jnp.int32)
    leaving = jnp.any(moving[None, :] == home_row[:, None], axis=1)
    matched = (destination[None, :] == owner_inst[:, None]) & (lane_index[None, :] == (within - R_DEV)[:, None])
    arriving = jnp.any(matched, axis=1) & jnp.logical_not(is_home)
    arrival_row = jnp.sum(jnp.where(matched, moving[None, :], 0), axis=1).astype(jnp.int32)
    arrival_length = jnp.sum(jnp.where(matched, base_length[None, :], 0), axis=1).astype(jnp.int32)
    arrival_done = jnp.sum(jnp.where(matched, done_round[None, :], 0), axis=1).astype(jnp.int32)
    slot_row = jnp.where(is_home, home_row, arrival_row).astype(jnp.int32)
    slot_length = jnp.where(is_home, jnp.take(lengths, home_row), jnp.where(arriving, arrival_length, 0)).astype(jnp.int32)
    step_round = jnp.arange(STEPS, dtype=jnp.int32) // ROUND_STEPS
    home_active = jnp.logical_not(leaving)[:, None] & (step_round[None, :] >= 0)
    arrival_active = arriving[:, None] & (step_round[None, :] > arrival_done[:, None])
    active = jnp.where(is_home[:, None], home_active, arrival_active)

    def per_slot(slot_items):
        row_index, length, active_steps, query_rows, fresh_rows = slot_items
        return attend_slot(kv_cache, row_index, length, active_steps, query_rows, fresh_rows)

    heads_out = lax.map(per_slot, (slot_row, slot_length, active, queries, fresh_kv))
    projected = jnp.dot(heads_out.reshape(INSTANCES * SLOTS * STEPS, HEADS * HEAD_DIM), out_proj, preferred_element_type=jnp.float32)
    projected = projected.reshape(INSTANCES * SLOTS, STEPS, OUT_COLS)
    attended = jnp.where(active[:, :, None], projected, 0.0).astype(jnp.bfloat16)

    lane_rows = slot_row.reshape(INSTANCES, SLOTS)[:, R_DEV:].reshape(-1)
    lane_lengths = slot_length.reshape(INSTANCES, SLOTS)[:, R_DEV:].reshape(-1)
    lane_active = active.reshape(INSTANCES, SLOTS, STEPS)[:, R_DEV:].reshape(-1, STEPS)
    lane_fresh = fresh_kv.reshape(INSTANCES, SLOTS, STEPS, -1)[:, R_DEV:].reshape(INSTANCES * ARRIVAL_SLOTS, STEPS, -1)

    def per_lane(lane_items):
        row_index, length, active_steps, fresh_rows = lane_items
        return land_slot(kv_cache, row_index, length, active_steps, fresh_rows)

    arrived_cache = lax.map(per_lane, (lane_rows, lane_lengths, lane_active, lane_fresh))
    return attended, arrived_cache
```

```python
import functools

import jax
import jax.numpy as jnp
from jax import lax
from jax.experimental import pallas as pl
from jax.experimental.pallas import tpu as pltpu
from jax.sharding import PartitionSpec as P

MESH = pl.DeviceIdType.MESH
HEAD_DIM = 128
R_DEV = 8
LANES = 4
DISTANCES = (1, 2, 8, 16)
INSTANCES = 32
TP = 8
CACHE = 2048
PAD_KEYS = 128
STEPS = 6
GROUP = 8
COLS = 512
CHUNK = 256
CHUNKS = CACHE // CHUNK
MASKED = -1e30
SCALE = HEAD_DIM**-0.5

RELAYS = (
    (0, 15, 0, 0, 1),
    (1, 10, 14, 12, 0),
    (1, 14, 1, 0, 1),
    (1, 15, 2, 1, 1),
    (2, 0, 12, 8, 0),
)
EXTRA_PAIRS = (
    (15, 0, 0),
    (10, 14, 0),
    (14, 1, 0),
    (15, 2, 0),
    (0, 12, 0),
    (1, 0, 1),
    (2, 1, 1),
    (12, 8, 0),
)


def softmax_rows(scores):
    top = jnp.max(scores, axis=-1, keepdims=True)
    grown = jnp.exp(scores - top)
    total = jnp.sum(grown, axis=-1, keepdims=True)
    return (grown / total).astype(jnp.bfloat16)


def dot_t(a, b):
    return lax.dot_general(a, b, (((1,), (1,)), ((), ())), preferred_element_type=jnp.float32)


def kernel(
    moving_ref, destination_ref, pages_ref, lengths_ref,
    kv_hbm, q_hbm, fresh_hbm, proj_hbm,
    att_ref, cache_ref,
    kv, send, relay, proj, q_v, fresh_v,
    ask_out, ask_in, head_out, head_in, q_f, fresh_f, ask_f, heads, part_out, part_in, result, stay,
    kv_sem, load_sem, bulk_send, bulk_recv, relay_recv, relay_send,
    ask_send, ask_recv, head_send, head_recv, part_send, part_recv,
):
    me = lax.axis_index("inst")
    tp = lax.axis_index("tp")
    half = me // 16
    place = me % 16

    small_loads = [
        pltpu.make_async_copy(q_hbm, q_v, load_sem.at[0]),
        pltpu.make_async_copy(fresh_hbm, fresh_v, load_sem.at[1]),
    ]
    for copy in small_loads:
        copy.start()
    kv_load = [
        pltpu.make_async_copy(kv_hbm.at[row], kv.at[row, pl.ds(0, CACHE)], kv_sem.at[row])
        for row in range(R_DEV)
    ]
    for copy in kv_load:
        copy.start()
    proj_load = pltpu.make_async_copy(proj_hbm, proj, load_sem.at[2])
    proj_load.start()

    barrier = pltpu.get_barrier_semaphore()

    def greet(inst, peer):
        pl.semaphore_signal(barrier, inc=1, device_id=(inst, peer), device_id_type=MESH)

    for distance in (1, 2, 8, 16, 24, 30, 31):
        greet(lax.rem(me + distance, INSTANCES), tp)
    for offset in range(1, TP):
        greet(me, lax.rem(tp + offset, TP))
    greeted = jnp.int32(7 + TP - 1)
    for first, second, flip in EXTRA_PAIRS:
        other_half = (1 - half if flip else half) * 16

        @pl.when(place == first)
        def _():
            greet(other_half + second, tp)

        @pl.when(place == second)
        def _():
            greet(other_half + first, tp)

        greeted = greeted + jnp.where((place == first) | (place == second), 1, 0)

    moving = moving_ref[...]
    destination = destination_ref[...]
    source = moving >> 3
    distance_all = (destination - source) & (INSTANCES - 1)
    code = lax.broadcasted_iota(jnp.int32, moving.shape, 1) * R_DEV + (moving & (R_DEV - 1))
    own_row, own_length, own_done, arrival_done = [], [], [], []

    def done_round(m):
        return jnp.where(pages_ref[m, 2] > 0, 2, jnp.where(pages_ref[m, 1] > 0, 1, 0))

    for lane in range(LANES):
        on_lane = distance_all == DISTANCES[lane]
        own = jnp.sum(jnp.where(on_lane & (source == me), code, 0))
        arriving = jnp.sum(jnp.where(on_lane & (destination == me), code, 0))
        row = own & (R_DEV - 1)
        own_row.append(row)
        own_length.append(lengths_ref[me * R_DEV + row])
        own_done.append(done_round(own >> 3))
        arrival_done.append(done_round(arriving >> 3))
    staying, stay_place = [], []
    count = jnp.int32(0)
    for row in range(R_DEV):
        gone = own_row[0] == row
        for lane in range(1, LANES):
            gone = gone | (own_row[lane] == row)
        stays = jnp.where(gone, 0, 1)
        staying.append(stays)
        stay_place.append(count)
        count = count + stays
    for index in range(R_DEV - LANES):
        chosen = jnp.int32(0)
        for row in range(R_DEV):
            chosen = jnp.where((staying[row] == 1) & (stay_place[row] == index), row, chosen)
        stay[index] = chosen

    for copy in small_loads:
        copy.wait()
    ask_f[...] = jnp.zeros_like(ask_f)
    for lane in range(LANES):
        queries = q_v[R_DEV + lane].astype(jnp.float32)
        for head in range(GROUP):
            ask_f[2 * head : 2 * head + 2, :] = queries[4:6, head * HEAD_DIM : (head + 1) * HEAD_DIM]
        fresh = fresh_v[R_DEV + lane].astype(jnp.float32)
        ask_f[16:22, :] = fresh[:, :HEAD_DIM]
        ask_f[32:38, :] = fresh[:, HEAD_DIM:]
        ask_out[lane] = ask_f[...].astype(jnp.bfloat16)

    fresh_f[...] = jnp.zeros_like(fresh_f)
    for row in range(R_DEV):
        fresh_f[0:STEPS, :] = fresh_v[row].astype(jnp.float32)
        kv[row, CACHE : CACHE + PAD_KEYS, :] = fresh_f[...].astype(jnp.bfloat16)

    for copy in kv_load:
        copy.wait()
    for lane in range(LANES):

        def move_part(part, carry, lane=lane):
            where = pl.ds(pl.multiple_of(part * CHUNK, CHUNK), CHUNK)
            send[lane, where, :] = kv[own_row[lane], where, :]
            return carry

        lax.fori_loop(0, CHUNKS, move_part, 0)

    pl.semaphore_wait(barrier, greeted)

    def ask_copy(lane):
        return pltpu.make_async_remote_copy(
            src_ref=ask_out.at[lane], dst_ref=ask_in.at[lane],
            send_sem=ask_send.at[lane], recv_sem=ask_recv.at[lane],
            device_id=(lax.rem(me + INSTANCES - DISTANCES[lane], INSTANCES), tp), device_id_type=MESH,
        )

    def head_copy(lane):
        return pltpu.make_async_remote_copy(
            src_ref=head_out.at[lane], dst_ref=head_in.at[lane],
            send_sem=head_send.at[lane], recv_sem=head_recv.at[lane],
            device_id=(lax.rem(me + DISTANCES[lane], INSTANCES), tp), device_id_type=MESH,
        )

    def bulk_copy(lane, first, rows):
        where = pl.ds(first, rows)
        return pltpu.make_async_remote_copy(
            src_ref=send.at[lane, where], dst_ref=cache_ref.at[lane, where],
            send_sem=bulk_send.at[lane], recv_sem=bulk_recv.at[lane],
            device_id=(lax.rem(me + DISTANCES[lane], INSTANCES), tp), device_id_type=MESH,
        )

    special = [jnp.int32(0) for _ in range(LANES)]
    relay_of = [me for _ in range(LANES)]
    is_relay = jnp.int32(0)
    relay_lane = jnp.int32(0)
    relay_final = me
    for lane, first, middle, final, flip in RELAYS:
        special[lane] = jnp.where(place == first, 1, special[lane])
        relay_of[lane] = jnp.where(place == first, half * 16 + middle, relay_of[lane])
        is_relay = jnp.where(place == middle, 1, is_relay)
        relay_lane = jnp.where(place == middle, lane, relay_lane)
        last = (1 - half if flip else half) * 16 + final
        relay_final = jnp.where(place == middle, last, relay_final)
    relayed_lanes = sorted({entry[0] for entry in RELAYS})

    def first_leg(lane, chunk):
        where = pl.ds(chunk * CHUNK, CHUNK)
        return pltpu.make_async_remote_copy(
            src_ref=send.at[lane, where], dst_ref=relay.at[where],
            send_sem=bulk_send.at[lane], recv_sem=relay_recv.at[chunk],
            device_id=(relay_of[lane], tp), device_id_type=MESH,
        )

    def second_leg(chunk):
        where = pl.ds(chunk * CHUNK, CHUNK)
        return pltpu.make_async_remote_copy(
            src_ref=relay.at[where], dst_ref=cache_ref.at[relay_lane, where],
            send_sem=relay_send.at[chunk], recv_sem=bulk_recv.at[relay_lane],
            device_id=(relay_final, tp), device_id_type=MESH,
        )

    def start_lane(lane, chunk):
        if lane in relayed_lanes:

            @pl.when(special[lane] == 1)
            def _():
                first_leg(lane, chunk).start()

            @pl.when(special[lane] == 0)
            def _():
                bulk_copy(lane, chunk * CHUNK, CHUNK).start()

        else:
            bulk_copy(lane, chunk * CHUNK, CHUNK).start()

    def forward(chunks):
        @pl.when(is_relay == 1)
        def _():
            for chunk in chunks:
                where = pl.ds(chunk * CHUNK, CHUNK)
                pltpu.make_async_remote_copy(
                    src_ref=relay.at[where], dst_ref=relay.at[where],
                    send_sem=relay_send.at[chunk], recv_sem=relay_recv.at[chunk],
                    device_id=(relay_final, tp), device_id_type=MESH,
                ).wait_recv()
                second_leg(chunk).start()

    for lane in range(LANES):
        ask_copy(lane).start()
    for chunk in range(CHUNKS - 1):
        for lane in range(LANES):
            start_lane(lane, chunk)

    position = lax.broadcasted_iota(jnp.int32, (CHUNK, 1), 0) + (CACHE - CHUNK)
    for lane in range(LANES):
        ask_copy(lane).wait_recv()
        fresh_key = ask_in[lane, 16:32, :].astype(jnp.float32)
        fresh_value = ask_in[lane, 32:48, :].astype(jnp.float32)
        length = own_length[lane]
        decodes = own_done[lane] < 2
        old = send[lane, CACHE - CHUNK : CACHE, :].astype(jnp.float32)
        for part, fresh in ((0, fresh_key), (1, fresh_value)):
            columns = slice(part * HEAD_DIM, (part + 1) * HEAD_DIM)
            new = jnp.where(position < length, old[:, columns], 0.0)
            new = jnp.where((position == length) & decodes, fresh[4:5, :], new)
            new = jnp.where((position == length + 1) & decodes, fresh[5:6, :], new)
            send[lane, CACHE - CHUNK : CACHE, columns] = new.astype(jnp.bfloat16)
        start_lane(lane, CHUNKS - 1)

    for lane in range(LANES):
        scores = dot_t(ask_in[lane, 0:16, :], send[lane, :, :HEAD_DIM]) * SCALE
        key_at = lax.broadcasted_iota(jnp.int32, scores.shape, 1)
        step = lax.broadcasted_iota(jnp.int32, scores.shape, 0) & 1
        scores = jnp.where(key_at <= own_length[lane] + step, scores, MASKED)
        mixed = jnp.dot(softmax_rows(scores), send[lane, :, HEAD_DIM:], preferred_element_type=jnp.float32)
        head_out[lane] = mixed.astype(jnp.bfloat16)
        head_copy(lane).start()

    forward(range(0, 2))

    q_f[...] = jnp.zeros_like(q_f)

    def home(index, carry):
        row = stay[index]
        length = lengths_ref[me * R_DEV + row]
        queries = q_v[row].astype(jnp.float32)
        for head in range(GROUP):
            q_f[8 * head : 8 * head + STEPS, :] = queries[:, head * HEAD_DIM : (head + 1) * HEAD_DIM]
        scores = dot_t(q_f[...].astype(jnp.bfloat16), kv[row, :, :HEAD_DIM]) * SCALE
        key_at = lax.broadcasted_iota(jnp.int32, scores.shape, 1)
        step = lax.broadcasted_iota(jnp.int32, scores.shape, 0) & 7
        seen = (key_at < length) | ((key_at >= CACHE) & (key_at - CACHE <= step))
        scores = jnp.where(seen, scores, MASKED)
        mixed = jnp.dot(softmax_rows(scores), kv[row, :, HEAD_DIM:], preferred_element_type=jnp.float32)
        for head in range(GROUP):
            heads[index, 0:STEPS, head * HEAD_DIM : (head + 1) * HEAD_DIM] = mixed[8 * head : 8 * head + STEPS, :]
        return carry

    lax.fori_loop(0, R_DEV - LANES, home, 0)

    forward(range(2, 5))

    for lane in range(LANES):
        head_copy(lane).wait_recv()
        arrived = head_in[lane].astype(jnp.float32)
        for head in range(GROUP):
            heads[lane, STEPS : STEPS + 2, head * HEAD_DIM : (head + 1) * HEAD_DIM] = arrived[2 * head : 2 * head + 2, :]

    proj_load.wait()
    rows = heads[...].reshape(R_DEV * LANES, GROUP * HEAD_DIM).astype(jnp.bfloat16)

    def part_copy(peer, slot):
        return pltpu.make_async_remote_copy(
            src_ref=part_out.at[peer], dst_ref=part_in.at[slot],
            send_sem=part_send.at[peer], recv_sem=part_recv.at[slot],
            device_id=(me, peer), device_id_type=MESH,
        )

    def project(peer):
        columns = pl.ds(pl.multiple_of(peer * COLS, COLS), COLS)
        return jnp.dot(rows, proj[:, columns], preferred_element_type=jnp.float32)

    def project_for(offset, carry):
        peer = lax.rem(tp + offset, TP)
        part_out[peer] = project(peer).astype(jnp.bfloat16)
        part_copy(peer, tp).start()
        return carry

    lax.fori_loop(1, TP, project_for, 0)
    total = project(tp)

    forward(range(5, CHUNKS))

    for offset in range(1, TP):
        peer = lax.rem(tp + offset, TP)
        part_copy(peer, peer).wait_recv()
        total = total + part_in[peer].astype(jnp.float32)
    result[...] = total.reshape(LANES, R_DEV, COLS)

    for row in range(R_DEV):
        found = result[jnp.minimum(stay_place[row], R_DEV - LANES - 1)]
        att_ref[row] = jnp.where(staying[row] == 1, found[0:STEPS, :], 0.0).astype(jnp.bfloat16)
    for lane in range(LANES):
        found = jnp.concatenate([jnp.zeros((4, COLS), jnp.float32), result[lane, STEPS : STEPS + 2, :]], axis=0)
        att_ref[R_DEV + lane] = jnp.where(arrival_done[lane] < 2, found, 0.0).astype(jnp.bfloat16)

    for lane in range(LANES):
        ask_copy(lane).wait_send()
        head_copy(lane).wait_send()
        bulk_copy(lane, 0, CACHE).wait_send()
    for offset in range(1, TP):
        part_copy(lax.rem(tp + offset, TP), tp).wait_send()

    @pl.when(is_relay == 1)
    def _():
        for chunk in range(CHUNKS):
            second_leg(chunk).wait_send()

    for lane in range(LANES):
        bulk_copy(lane, 0, CACHE).wait_recv()


def local(kv_cache, queries, fresh_kv, out_proj, moving, destination, round_pages, lengths):
    bf16, f32 = jnp.bfloat16, jnp.float32
    row_width = kv_cache.shape[2]
    dma = pltpu.SemaphoreType.DMA
    any_space = pl.BlockSpec(memory_space=pl.ANY)
    smem = pl.BlockSpec(memory_space=pltpu.SMEM)
    vmem = pl.BlockSpec(memory_space=pltpu.VMEM)
    slots = R_DEV + LANES
    attended, arrived = pl.pallas_call(
        kernel,
        out_shape=(
            jax.ShapeDtypeStruct((slots, STEPS, COLS), bf16),
            jax.ShapeDtypeStruct((LANES, CACHE, row_width), bf16),
        ),
        in_specs=[vmem, vmem, smem, smem, any_space, any_space, any_space, any_space],
        out_specs=(vmem, any_space),
        scratch_shapes=[
            pltpu.VMEM((R_DEV, CACHE + PAD_KEYS, row_width), bf16),
            pltpu.VMEM((LANES, CACHE, row_width), bf16),
            pltpu.VMEM((CACHE, row_width), bf16),
            pltpu.VMEM(out_proj.shape, bf16),
            pltpu.VMEM(queries.shape, bf16),
            pltpu.VMEM(fresh_kv.shape, bf16),
            pltpu.VMEM((LANES, 48, HEAD_DIM), bf16),
            pltpu.VMEM((LANES, 48, HEAD_DIM), bf16),
            pltpu.VMEM((LANES, 16, HEAD_DIM), bf16),
            pltpu.VMEM((LANES, 16, HEAD_DIM), bf16),
            pltpu.VMEM((8 * GROUP, HEAD_DIM), f32),
            pltpu.VMEM((PAD_KEYS, row_width), f32),
            pltpu.VMEM((48, HEAD_DIM), f32),
            pltpu.VMEM((LANES, R_DEV, GROUP * HEAD_DIM), f32),
            pltpu.VMEM((TP, LANES * R_DEV, COLS), bf16),
            pltpu.VMEM((TP, LANES * R_DEV, COLS), bf16),
            pltpu.VMEM((LANES, R_DEV, COLS), f32),
            pltpu.SMEM((R_DEV - LANES,), jnp.int32),
            dma((R_DEV,)),
            dma((3,)),
            dma((LANES,)),
            dma((LANES,)),
            dma((CHUNKS,)),
            dma((CHUNKS,)),
            dma((LANES,)),
            dma((LANES,)),
            dma((LANES,)),
            dma((LANES,)),
            dma((TP,)),
            dma((TP,)),
        ],
        compiler_params=pltpu.CompilerParams(
            collective_id=0, has_side_effects=True, vmem_limit_bytes=48 * 2**20
        ),
    )(
        moving.reshape(1, -1), destination.reshape(1, -1), round_pages, lengths,
        kv_cache, queries, fresh_kv, out_proj,
    )
    return attended, arrived


def solution(mesh):
    in_specs = (
        P("inst", None, "tp"),
        P("inst", None, "tp"),
        P("inst", None, "tp"),
        P("tp", None),
        P(),
        P(),
        P(),
        P(),
    )
    out_specs = (P("inst", None, "tp"), P("inst", None, "tp"))
    return jax.shard_map(local, mesh=mesh, in_specs=in_specs, out_specs=out_specs, check_vma=False)
```

```python
import functools

import jax
import jax.numpy as jnp
from jax import lax
from jax.experimental import pallas as pl
from jax.experimental.pallas import tpu as pltpu
from jax.sharding import PartitionSpec as P

MESH = pl.DeviceIdType.MESH
HEAD_DIM = 128
R_DEV = 8
LANES = 4
DISTANCES = (1, 2, 8, 16)
INSTANCES = 32
TP = 8
CACHE = 2048
PAD_KEYS = 128
STEPS = 6
GROUP = 8
COLS = 512
CHUNK = 128
CHUNKS = CACHE // CHUNK
TAIL = 256
DEPTH = 3
LAG = 5
HOPS = (2, 1, 3, 0)
PACE = ((3, 3), (3, 4), (4, 4), (4, 5), (5, 6), (6, 6), (6, 7), (7, 8), (8, 8), (8, 8), (8, 9), (9, 9), (9, 9), (9, 10), (10, 10), (10, 10), (10, 11), (11, 16))
MASKED = -1e30
SCALE = HEAD_DIM**-0.5

RELAYS = (
    (0, 15, 0, 0, 0, 12),
    (1, 0, 3, 0, 0, 4),
    (1, 2, 6, 0, 0, 8),
    (1, 4, 7, 0, 0, 4),
    (1, 6, 10, 0, 0, 12),
    (1, 8, 11, 0, 0, 4),
    (1, 10, 9, 0, 0, 8),
    (1, 10, 14, 0, 8, 16),
    (1, 12, 15, 0, 0, 4),
    (1, 14, 1, 0, 0, 12),
    (1, 15, 2, 0, 0, 12),
    (2, 0, 12, 0, 0, 12),
    (2, 1, 13, 0, 0, 4),
    (2, 8, 4, 0, 0, 12),
    (2, 9, 5, 0, 0, 4),
    (2, 10, 6, 0, 0, 4),
    (2, 11, 3, 0, 0, 4),
    (2, 12, 8, 0, 0, 4),
    (2, 13, 5, 0, 0, 4),
    (2, 14, 6, 0, 0, 8),
    (2, 15, 7, 0, 0, 12),
)


def relay_plan():
    plan, slots = {}, {}
    for lane, source, middle, flip, first, last in RELAYS:
        for chunk in range(first, last):
            plan.setdefault(middle, []).append((chunk * CHUNK, lane, source, flip))
    for middle in plan:
        plan[middle].sort()
        for slot, (row, lane, source, flip) in enumerate(plan[middle]):
            slots[middle, lane, source, row] = slot
    base = {(d, 0) for d in DISTANCES} | {(INSTANCES - d, 0) for d in DISTANCES}
    pairs = []

    def meet(first, second, flip):
        shift_a = (second + 16 * flip - first) % INSTANCES
        shift_b = (second - first - 16 * flip) % INSTANCES
        known = all((shift, 0) in base for shift in (shift_a, shift_b))
        entry, back = (first, second, flip), (second, first, flip)
        if not known and entry not in pairs and back not in pairs:
            pairs.append(entry)

    for lane, source, middle, flip, first, last in RELAYS:
        meet(source, middle, flip)
        final = source + DISTANCES[lane]
        meet(middle, final % 16, (flip + final // 16) % 2)
    return plan, slots, tuple(pairs)


RELAY_PLAN, RELAY_SLOTS, EXTRA_PAIRS = relay_plan()
RELAY_PIECES = max([len(pieces) for pieces in RELAY_PLAN.values()], default=1)


def softmax_rows(scores):
    top = jnp.max(scores, axis=-1, keepdims=True)
    grown = jnp.exp(scores - top)
    total = jnp.sum(grown, axis=-1, keepdims=True)
    return (grown * (1.0 / total)).astype(jnp.bfloat16)


def dot_t(a, b):
    return lax.dot_general(a, b, (((1,), (1,)), ((), ())), preferred_element_type=jnp.float32)


def kernel(
    moving_hbm, destination_hbm, pages_hbm, lengths_hbm,
    kv_hbm, q_hbm, fresh_hbm, proj_hbm,
    att_ref, cache_ref,
    kv, send, relay, proj, q_v, fresh_v,
    moving_ref, destination_ref, pages_ref, lengths_ref,
    ask_out, ask_in, head_out, head_in, q_f, fresh_f, ask_f, heads, pair_out, pair_in, part_out, part_in, result, stay,
    kv_sem, load_sem, bulk_send, bulk_recv, relay_recv, relay_send,
    ask_send, ask_recv, head_send, head_recv, pair_send, pair_recv, part_send, part_recv,
):
    me = lax.axis_index("inst")
    tp = lax.axis_index("tp")
    half = me // 16
    place = me % 16

    plan_loads = [
        pltpu.make_async_copy(moving_hbm, moving_ref, load_sem.at[3]),
        pltpu.make_async_copy(destination_hbm, destination_ref, load_sem.at[4]),
        pltpu.make_async_copy(pages_hbm, pages_ref, load_sem.at[5]),
        pltpu.make_async_copy(lengths_hbm, lengths_ref, load_sem.at[6]),
    ]
    small_loads = [
        pltpu.make_async_copy(q_hbm, q_v, load_sem.at[0]),
        pltpu.make_async_copy(fresh_hbm, fresh_v, load_sem.at[1]),
    ]
    kv_load = [
        pltpu.make_async_copy(kv_hbm.at[row], kv.at[row, pl.ds(0, CACHE)], kv_sem.at[row])
        for row in range(R_DEV)
    ]
    proj_load = pltpu.make_async_copy(proj_hbm, proj, load_sem.at[2])
    for copy in plan_loads + small_loads + kv_load:
        copy.start()

    barrier = pltpu.get_barrier_semaphore()

    def greet(inst, peer):
        pl.semaphore_signal(barrier, inc=1, device_id=(inst, peer), device_id_type=MESH)

    for distance in (1, 2, 8, 16, 24, 30, 31):
        greet(lax.rem(me + distance, INSTANCES), tp)
    core = tp % 2
    sibling = tp + 1 - 2 * core
    greet(me, sibling)
    for hop in range(1, TP // 2):
        greet(me, lax.rem(tp + 2 * hop, TP))
    greeted = jnp.int32(7 + TP // 2)
    for first, second, flip in EXTRA_PAIRS:
        other_half = (1 - half if flip else half) * 16

        @pl.when(place == first)
        def _():
            greet(other_half + second, tp)

        @pl.when(place == second)
        def _():
            greet(other_half + first, tp)

        greeted = greeted + jnp.where((place == first) | (place == second), 1, 0)

    for copy in plan_loads:
        copy.wait()
    moving = moving_ref[...]
    destination = destination_ref[...]
    source = moving >> 3
    distance_all = (destination - source) & (INSTANCES - 1)
    code = lax.broadcasted_iota(jnp.int32, moving.shape, 1) * R_DEV + (moving & (R_DEV - 1))
    own_row, own_length, own_done, arrival_done = [], [], [], []

    def done_round(m):
        return jnp.where(pages_ref[2, m] > 0, 2, jnp.where(pages_ref[1, m] > 0, 1, 0))

    for lane in range(LANES):
        on_lane = distance_all == DISTANCES[lane]
        own = jnp.sum(jnp.where(on_lane & (source == me), code, 0))
        arriving = jnp.sum(jnp.where(on_lane & (destination == me), code, 0))
        row = own & (R_DEV - 1)
        own_row.append(row)
        own_length.append(lengths_ref[me * R_DEV + row])
        own_done.append(done_round(own >> 3))
        arrival_done.append(done_round(arriving >> 3))
    staying, stay_place = [], []
    count = jnp.int32(0)
    for row in range(R_DEV):
        gone = own_row[0] == row
        for lane in range(1, LANES):
            gone = gone | (own_row[lane] == row)
        stays = jnp.where(gone, 0, 1)
        staying.append(stays)
        stay_place.append(count)
        count = count + stays
    for index in range(R_DEV - LANES):
        chosen = jnp.int32(0)
        for row in range(R_DEV):
            chosen = jnp.where((staying[row] == 1) & (stay_place[row] == index), row, chosen)
        stay[index] = chosen

    for copy in small_loads:
        copy.wait()
    ask_f[...] = jnp.zeros_like(ask_f)
    for lane in range(LANES):
        queries = q_v[R_DEV + lane].astype(jnp.float32)
        for head in range(GROUP):
            ask_f[2 * head : 2 * head + 2, :] = queries[4:6, head * HEAD_DIM : (head + 1) * HEAD_DIM]
        fresh = fresh_v[R_DEV + lane].astype(jnp.float32)
        ask_f[16:22, :] = fresh[:, :HEAD_DIM]
        ask_f[32:38, :] = fresh[:, HEAD_DIM:]
        ask_out[lane] = ask_f[...].astype(jnp.bfloat16)

    for copy in kv_load:
        copy.wait()
    for lane in range(LANES):

        def move_part(part, carry, lane=lane):
            where = pl.ds(pl.multiple_of(part * TAIL, TAIL), TAIL)
            send[lane, where, :] = kv[own_row[lane], where, :]
            return carry

        lax.fori_loop(0, CACHE // TAIL, move_part, 0)

    pl.semaphore_wait(barrier, greeted)

    def ask_copy(lane):
        return pltpu.make_async_remote_copy(
            src_ref=ask_out.at[lane], dst_ref=ask_in.at[lane],
            send_sem=ask_send.at[lane], recv_sem=ask_recv.at[lane],
            device_id=(lax.rem(me + INSTANCES - DISTANCES[lane], INSTANCES), tp), device_id_type=MESH,
        )

    def head_copy(lane):
        return pltpu.make_async_remote_copy(
            src_ref=head_out.at[lane], dst_ref=head_in.at[lane],
            send_sem=head_send.at[lane], recv_sem=head_recv.at[lane],
            device_id=(lax.rem(me + DISTANCES[lane], INSTANCES), tp), device_id_type=MESH,
        )

    def bulk_copy(lane, first, rows):
        where = pl.ds(first, rows)
        return pltpu.make_async_remote_copy(
            src_ref=send.at[lane, where], dst_ref=cache_ref.at[lane, where],
            send_sem=bulk_send.at[lane, first // CHUNK], recv_sem=bulk_recv.at[lane],
            device_id=(lax.rem(me + DISTANCES[lane], INSTANCES), tp), device_id_type=MESH,
        )

    def first_leg(lane, source, middle, flip, row):
        slot = RELAY_SLOTS[middle, lane, source, row]
        return pltpu.make_async_remote_copy(
            src_ref=send.at[lane, pl.ds(row, CHUNK)], dst_ref=relay.at[pl.ds(slot * CHUNK, CHUNK)],
            send_sem=bulk_send.at[lane, row // CHUNK], recv_sem=relay_recv.at[slot],
            device_id=((1 - half if flip else half) * 16 + middle, tp), device_id_type=MESH,
        )

    def second_leg(slot, row, lane, source, flip):
        origin = (1 - half if flip else half) * 16 + source
        return pltpu.make_async_remote_copy(
            src_ref=relay.at[pl.ds(slot * CHUNK, CHUNK)], dst_ref=cache_ref.at[lane, pl.ds(row, CHUNK)],
            send_sem=relay_send.at[slot], recv_sem=bulk_recv.at[lane],
            device_id=(lax.rem(origin + DISTANCES[lane], INSTANCES), tp), device_id_type=MESH,
        )

    def landed(slot):
        piece = relay.at[pl.ds(slot * CHUNK, CHUNK)]
        return pltpu.make_async_remote_copy(
            src_ref=piece, dst_ref=piece, send_sem=relay_send.at[slot], recv_sem=relay_recv.at[slot],
            device_id=(lax.rem(me + 1, INSTANCES), tp), device_id_type=MESH,
        )

    def start_lane(lane, chunk):
        direct = None
        for relayed, source, middle, flip, first, last in RELAYS:
            if relayed == lane and first <= chunk < last:

                @pl.when(place == source)
                def _():
                    first_leg(lane, source, middle, flip, chunk * CHUNK).start()

                here = place != source
                direct = here if direct is None else direct & here
        if direct is None:
            bulk_copy(lane, chunk * CHUNK, CHUNK).start()
        else:

            @pl.when(direct)
            def _():
                bulk_copy(lane, chunk * CHUNK, CHUNK).start()

    def forward(chunk):
        for middle, pieces in RELAY_PLAN.items():
            due = [slot for slot in range(len(pieces)) if pieces[slot][0] == chunk * CHUNK]
            if due:

                @pl.when(place == middle)
                def _():
                    for slot in due:
                        landed(slot).wait_recv()
                        second_leg(slot, *pieces[slot]).start()

    def migrate(first, last):
        for step in range(first, last):
            if step < CHUNKS:
                for lane in range(LANES):
                    if step >= DEPTH:
                        bulk_copy(lane, (step - DEPTH) * CHUNK, CHUNK).wait_send()
                    start_lane(lane, step)
            if step >= LAG:
                forward(step - LAG)

    for lane in range(LANES):
        ask_copy(lane).start()
    migrate(0, DEPTH)
    proj_load.start()

    position = lax.broadcasted_iota(jnp.int32, (TAIL, 1), 0) + (CACHE - TAIL)
    for lane in range(LANES):
        ask_copy(lane).wait_recv()
        fresh_key = ask_in[lane, 16:32, :].astype(jnp.float32)
        fresh_value = ask_in[lane, 32:48, :].astype(jnp.float32)
        length = own_length[lane]
        decodes = own_done[lane] < 2
        old = send[lane, CACHE - TAIL : CACHE, :].astype(jnp.float32)
        for part, fresh in ((0, fresh_key), (1, fresh_value)):
            columns = slice(part * HEAD_DIM, (part + 1) * HEAD_DIM)
            new = jnp.where(position < length, old[:, columns], 0.0)
            new = jnp.where((position == length) & decodes, fresh[4:5, :], new)
            new = jnp.where((position == length + 1) & decodes, fresh[5:6, :], new)
            send[lane, CACHE - TAIL : CACHE, columns] = new.astype(jnp.bfloat16)

    for lane in range(LANES):
        scores = dot_t(ask_in[lane, 0:16, :], send[lane, :, :HEAD_DIM]) * SCALE
        key_at = lax.broadcasted_iota(jnp.int32, scores.shape, 1)
        step = lax.broadcasted_iota(jnp.int32, scores.shape, 0) & 1
        scores = jnp.where(key_at <= own_length[lane] + step, scores, MASKED)
        mixed = jnp.dot(softmax_rows(scores), send[lane, :, HEAD_DIM:], preferred_element_type=jnp.float32)
        head_out[lane] = mixed.astype(jnp.bfloat16)
        head_copy(lane).start()
        migrate(*PACE[lane])

    fresh_f[...] = jnp.zeros_like(fresh_f)
    for row in range(R_DEV):
        fresh_f[0:STEPS, :] = fresh_v[row].astype(jnp.float32)
        kv[row, CACHE : CACHE + PAD_KEYS, :] = fresh_f[...].astype(jnp.bfloat16)

    q_f[...] = jnp.zeros_like(q_f)

    def home(index):
        row = stay[index]
        length = lengths_ref[me * R_DEV + row]
        queries = q_v[row].astype(jnp.float32)
        for head in range(GROUP):
            q_f[8 * head : 8 * head + STEPS, :] = queries[:, head * HEAD_DIM : (head + 1) * HEAD_DIM]
        scores = dot_t(q_f[...].astype(jnp.bfloat16), kv[row, :, :HEAD_DIM]) * SCALE
        key_at = lax.broadcasted_iota(jnp.int32, scores.shape, 1)
        step = lax.broadcasted_iota(jnp.int32, scores.shape, 0) & 7
        seen = (key_at < length) | ((key_at >= CACHE) & (key_at - CACHE <= step))
        scores = jnp.where(seen, scores, MASKED)
        mixed = jnp.dot(softmax_rows(scores), kv[row, :, HEAD_DIM:], preferred_element_type=jnp.float32)
        for head in range(GROUP):
            heads[index, 0:STEPS, head * HEAD_DIM : (head + 1) * HEAD_DIM] = mixed[8 * head : 8 * head + STEPS, :]

    for index in range(R_DEV - LANES):
        home(index)
        migrate(*PACE[4 + index])

    migrate(*PACE[8])
    for lane in range(LANES):
        head_copy(lane).wait_recv()
        arrived = head_in[lane].astype(jnp.float32)
        for head in range(GROUP):
            heads[lane, STEPS : STEPS + 2, head * HEAD_DIM : (head + 1) * HEAD_DIM] = arrived[2 * head : 2 * head + 2, :]

    proj_load.wait()
    rows = heads[...].reshape(R_DEV * LANES, GROUP * HEAD_DIM).astype(jnp.bfloat16)

    def pair_copy(hop):
        return pltpu.make_async_remote_copy(
            src_ref=pair_out.at[hop], dst_ref=pair_in.at[hop],
            send_sem=pair_send.at[hop], recv_sem=pair_recv.at[hop],
            device_id=(me, sibling), device_id_type=MESH,
        )

    def part_copy(hop):
        return pltpu.make_async_remote_copy(
            src_ref=part_out.at[hop], dst_ref=part_in.at[hop],
            send_sem=part_send.at[hop], recv_sem=part_recv.at[hop],
            device_id=(me, lax.rem(tp + 2 * hop, TP)), device_id_type=MESH,
        )

    def project(peer):
        columns = pl.ds(pl.multiple_of(peer * COLS, COLS), COLS)
        return jnp.dot(rows, proj[:, columns], preferred_element_type=jnp.float32)

    for index, hop in enumerate(HOPS):
        pair_out[hop] = project(lax.rem(sibling + 2 * hop, TP))
        pair_copy(hop).start()
        migrate(*PACE[9 + index])
    total = None
    for index, hop in enumerate(HOPS):
        mine = project(lax.rem(tp + 2 * hop, TP))
        pair_copy(hop).wait_recv()
        mine = mine + pair_in[hop]
        if hop:
            part_out[hop] = mine.astype(jnp.bfloat16)
            part_copy(hop).start()
        else:
            total = mine
        migrate(*PACE[13 + index])

    migrate(*PACE[17])
    for hop in HOPS[:-1]:
        part_copy(hop).wait_recv()
        total = total + part_in[hop].astype(jnp.float32)
    result[...] = total.reshape(LANES, R_DEV, COLS)

    for row in range(R_DEV):
        found = result[jnp.minimum(stay_place[row], R_DEV - LANES - 1)]
        att_ref[row] = jnp.where(staying[row] == 1, found[0:STEPS, :], 0.0).astype(jnp.bfloat16)
    for lane in range(LANES):
        found = jnp.concatenate([jnp.zeros((4, COLS), jnp.float32), result[lane, STEPS : STEPS + 2, :]], axis=0)
        att_ref[R_DEV + lane] = jnp.where(arrival_done[lane] < 2, found, 0.0).astype(jnp.bfloat16)

    migrate(PACE[17][1], CHUNKS + LAG)

    for lane in range(LANES):
        ask_copy(lane).wait_send()
        head_copy(lane).wait_send()
        for chunk in range(CHUNKS - DEPTH, CHUNKS):
            bulk_copy(lane, chunk * CHUNK, CHUNK).wait_send()
    for hop in HOPS:
        pair_copy(hop).wait_send()
        if hop:
            part_copy(hop).wait_send()

    for middle, pieces in RELAY_PLAN.items():

        @pl.when(place == middle)
        def _():
            for slot, piece in enumerate(pieces):
                second_leg(slot, *piece).wait_send()

    for lane in range(LANES):
        bulk_copy(lane, 0, CACHE).wait_recv()


def local(kv_cache, queries, fresh_kv, out_proj, moving, destination, round_pages, lengths):
    bf16, f32 = jnp.bfloat16, jnp.float32
    row_width = kv_cache.shape[2]
    dma = pltpu.SemaphoreType.DMA
    hbm = pl.BlockSpec(memory_space=pltpu.HBM)
    vmem = pl.BlockSpec(memory_space=pltpu.VMEM)
    slots = R_DEV + LANES
    attended, arrived = pl.pallas_call(
        kernel,
        out_shape=(
            pltpu.VMEM((slots, STEPS, COLS), bf16),
            pltpu.VMEM((LANES, CACHE, row_width), bf16),
        ),
        in_specs=[hbm] * 8,
        out_specs=(vmem, vmem),
        scratch_shapes=[
            pltpu.VMEM((R_DEV, CACHE + PAD_KEYS, row_width), bf16),
            pltpu.VMEM((LANES, CACHE, row_width), bf16),
            pltpu.VMEM((RELAY_PIECES * CHUNK, row_width), bf16),
            pltpu.VMEM(out_proj.shape, bf16),
            pltpu.VMEM(queries.shape, bf16),
            pltpu.VMEM(fresh_kv.shape, bf16),
            pltpu.VMEM((1, moving.shape[0]), jnp.int32),
            pltpu.VMEM((1, moving.shape[0]), jnp.int32),
            pltpu.SMEM((round_pages.shape[1], round_pages.shape[0]), jnp.int32),
            pltpu.SMEM(lengths.shape, jnp.int32),
            pltpu.VMEM((LANES, 48, HEAD_DIM), bf16),
            pltpu.VMEM((LANES, 48, HEAD_DIM), bf16),
            pltpu.VMEM((LANES, 16, HEAD_DIM), bf16),
            pltpu.VMEM((LANES, 16, HEAD_DIM), bf16),
            pltpu.VMEM((8 * GROUP, HEAD_DIM), f32),
            pltpu.VMEM((PAD_KEYS, row_width), f32),
            pltpu.VMEM((48, HEAD_DIM), f32),
            pltpu.VMEM((LANES, R_DEV, GROUP * HEAD_DIM), f32),
            pltpu.VMEM((TP // 2, LANES * R_DEV, COLS), f32),
            pltpu.VMEM((TP // 2, LANES * R_DEV, COLS), f32),
            pltpu.VMEM((TP // 2, LANES * R_DEV, COLS), bf16),
            pltpu.VMEM((TP // 2, LANES * R_DEV, COLS), bf16),
            pltpu.VMEM((LANES, R_DEV, COLS), f32),
            pltpu.SMEM((R_DEV - LANES,), jnp.int32),
            dma((R_DEV,)),
            dma((7,)),
            dma((LANES, CHUNKS)),
            dma((LANES,)),
            dma((RELAY_PIECES,)),
            dma((RELAY_PIECES,)),
            dma((LANES,)),
            dma((LANES,)),
            dma((LANES,)),
            dma((LANES,)),
            dma((TP // 2,)),
            dma((TP // 2,)),
            dma((TP // 2,)),
            dma((TP // 2,)),
        ],
        compiler_params=pltpu.CompilerParams(
            collective_id=0, has_side_effects=True, vmem_limit_bytes=40 * 2**20
        ),
    )(
        *(
            pltpu.with_memory_space_constraint(operand, pltpu.HBM)
            for operand in (
                moving.reshape(1, -1), destination.reshape(1, -1), round_pages.T, lengths,
                kv_cache, queries, fresh_kv, out_proj,
            )
        )
    )
    return attended, arrived


def solution(mesh):
    in_specs = (
        P("inst", None, "tp"),
        P("inst", None, "tp"),
        P("inst", None, "tp"),
        P("tp", None),
        P(),
        P(),
        P(),
        P(),
    )
    out_specs = (P("inst", None, "tp"), P("inst", None, "tp"))
    return jax.shard_map(local, mesh=mesh, in_specs=in_specs, out_specs=out_specs, check_vma=False)
```

```python
import functools

import jax
import jax.numpy as jnp
from jax import lax
from jax.experimental import pallas as pl
from jax.experimental.pallas import tpu as pltpu
from jax.sharding import PartitionSpec as P

MESH = pl.DeviceIdType.MESH
HEAD_DIM = 128
R_DEV = 8
LANES = 4
DISTANCES = (1, 2, 8, 16)
INSTANCES = 32
TP = 8
CACHE = 2048
PAD_KEYS = 128
STEPS = 6
GROUP = 8
COLS = 512
CHUNK = 128
CHUNKS = CACHE // CHUNK
TAIL = 256
DEPTH = 3
LAG = 5
HOPS = (2, 1, 3, 0)
PACE = ((3, 3), (3, 4), (4, 4), (4, 5), (5, 6), (6, 6), (6, 7), (7, 8), (8, 8), (8, 8), (8, 9), (9, 9), (9, 9), (9, 10), (10, 10), (10, 10), (10, 11), (11, 16))
MASKED = -1e30
SCALE = HEAD_DIM**-0.5

RELAYS = (
    (0, 7, 11, 0, 0, 4),
    (0, 15, 0, 0, 0, 4),
    (0, 15, 3, 0, 4, 8),
    (1, 0, 3, 0, 0, 4),
    (1, 2, 5, 0, 0, 4),
    (1, 2, 7, 0, 4, 8),
    (1, 4, 7, 0, 0, 4),
    (1, 6, 9, 0, 0, 4),
    (1, 8, 11, 0, 0, 4),
    (1, 10, 14, 0, 0, 4),
    (1, 10, 15, 0, 4, 8),
    (1, 12, 15, 0, 0, 4),
    (1, 14, 1, 0, 0, 8),
    (1, 15, 1, 0, 0, 4),
    (1, 15, 2, 0, 4, 12),
    (2, 0, 12, 0, 0, 12),
    (2, 1, 13, 0, 0, 8),
    (2, 8, 4, 0, 0, 12),
    (2, 9, 5, 0, 0, 4),
    (2, 10, 2, 0, 0, 4),
    (2, 11, 7, 0, 0, 4),
    (2, 12, 8, 0, 0, 4),
    (2, 13, 5, 0, 0, 4),
    (2, 14, 6, 0, 0, 12),
    (2, 15, 3, 0, 0, 8),
    (2, 15, 7, 0, 8, 16),
)


def relay_plan():
    plan, slots = {}, {}
    for lane, source, middle, flip, first, last in RELAYS:
        for chunk in range(first, last):
            plan.setdefault(middle, []).append((chunk * CHUNK, lane, source, flip))
    for middle in plan:
        plan[middle].sort()
        for slot, (row, lane, source, flip) in enumerate(plan[middle]):
            slots[middle, lane, source, row] = slot
    base = {(d, 0) for d in DISTANCES} | {(INSTANCES - d, 0) for d in DISTANCES}
    pairs = []

    def meet(first, second, flip):
        shift_a = (second + 16 * flip - first) % INSTANCES
        shift_b = (second - first - 16 * flip) % INSTANCES
        known = all((shift, 0) in base for shift in (shift_a, shift_b))
        entry, back = (first, second, flip), (second, first, flip)
        if not known and entry not in pairs and back not in pairs:
            pairs.append(entry)

    for lane, source, middle, flip, first, last in RELAYS:
        meet(source, middle, flip)
        final = source + DISTANCES[lane]
        meet(middle, final % 16, (flip + final // 16) % 2)
    return plan, slots, tuple(pairs)


RELAY_PLAN, RELAY_SLOTS, EXTRA_PAIRS = relay_plan()
RELAY_PIECES = max([len(pieces) for pieces in RELAY_PLAN.values()], default=1)


def softmax_rows(scores):
    top = jnp.max(scores, axis=-1, keepdims=True)
    grown = jnp.exp(scores - top)
    total = jnp.sum(grown, axis=-1, keepdims=True)
    return (grown * (1.0 / total)).astype(jnp.bfloat16)


def dot_t(a, b):
    return lax.dot_general(a, b, (((1,), (1,)), ((), ())), preferred_element_type=jnp.float32)


def kernel(
    moving_hbm, destination_hbm, pages_hbm, lengths_hbm,
    kv_hbm, q_hbm, fresh_hbm, proj_hbm,
    att_ref, cache_ref,
    kv, send, relay, proj, q_v, fresh_v,
    moving_ref, destination_ref, pages_ref, lengths_ref,
    ask_out, ask_in, head_out, head_in, q_f, fresh_f, ask_f, heads, pair_out, pair_in, part_out, part_in, result, stay,
    kv_sem, load_sem, bulk_send, bulk_recv, relay_recv, relay_send,
    ask_send, ask_recv, head_send, head_recv, pair_send, pair_recv, part_send, part_recv,
):
    me = lax.axis_index("inst")
    tp = lax.axis_index("tp")
    half = me // 16
    place = me % 16

    plan_loads = [
        pltpu.make_async_copy(moving_hbm, moving_ref, load_sem.at[3]),
        pltpu.make_async_copy(destination_hbm, destination_ref, load_sem.at[4]),
        pltpu.make_async_copy(pages_hbm, pages_ref, load_sem.at[5]),
        pltpu.make_async_copy(lengths_hbm, lengths_ref, load_sem.at[6]),
    ]
    small_loads = [
        pltpu.make_async_copy(q_hbm, q_v, load_sem.at[0]),
        pltpu.make_async_copy(fresh_hbm, fresh_v, load_sem.at[1]),
    ]
    kv_load = [
        pltpu.make_async_copy(kv_hbm.at[row], kv.at[row, pl.ds(0, CACHE)], kv_sem.at[row])
        for row in range(R_DEV)
    ]
    proj_load = pltpu.make_async_copy(proj_hbm, proj, load_sem.at[2])
    for copy in plan_loads + small_loads + kv_load:
        copy.start()

    barrier = pltpu.get_barrier_semaphore()

    def greet(inst, peer):
        pl.semaphore_signal(barrier, inc=1, device_id=(inst, peer), device_id_type=MESH)

    for distance in (1, 2, 8, 16, 24, 30, 31):
        greet(lax.rem(me + distance, INSTANCES), tp)
    core = tp % 2
    sibling = tp + 1 - 2 * core
    greet(me, sibling)
    for hop in range(1, TP // 2):
        greet(me, lax.rem(tp + 2 * hop, TP))
    greeted = jnp.int32(7 + TP // 2)
    for first, second, flip in EXTRA_PAIRS:
        other_half = (1 - half if flip else half) * 16

        @pl.when(place == first)
        def _():
            greet(other_half + second, tp)

        @pl.when(place == second)
        def _():
            greet(other_half + first, tp)

        greeted = greeted + jnp.where((place == first) | (place == second), 1, 0)

    for copy in plan_loads:
        copy.wait()
    moving = moving_ref[...]
    destination = destination_ref[...]
    source = moving >> 3
    distance_all = (destination - source) & (INSTANCES - 1)
    code = lax.broadcasted_iota(jnp.int32, moving.shape, 1) * R_DEV + (moving & (R_DEV - 1))
    own_row, own_length, own_done, arrival_done = [], [], [], []

    def done_round(m):
        return jnp.where(pages_ref[2, m] > 0, 2, jnp.where(pages_ref[1, m] > 0, 1, 0))

    for lane in range(LANES):
        on_lane = distance_all == DISTANCES[lane]
        own = jnp.sum(jnp.where(on_lane & (source == me), code, 0))
        arriving = jnp.sum(jnp.where(on_lane & (destination == me), code, 0))
        row = own & (R_DEV - 1)
        own_row.append(row)
        own_length.append(lengths_ref[me * R_DEV + row])
        own_done.append(done_round(own >> 3))
        arrival_done.append(done_round(arriving >> 3))
    staying, stay_place = [], []
    count = jnp.int32(0)
    for row in range(R_DEV):
        gone = own_row[0] == row
        for lane in range(1, LANES):
            gone = gone | (own_row[lane] == row)
        stays = jnp.where(gone, 0, 1)
        staying.append(stays)
        stay_place.append(count)
        count = count + stays
    for index in range(R_DEV - LANES):
        chosen = jnp.int32(0)
        for row in range(R_DEV):
            chosen = jnp.where((staying[row] == 1) & (stay_place[row] == index), row, chosen)
        stay[index] = chosen

    for copy in small_loads:
        copy.wait()
    ask_f[...] = jnp.zeros_like(ask_f)
    for lane in range(LANES):
        queries = q_v[R_DEV + lane].astype(jnp.float32)
        for head in range(GROUP):
            ask_f[2 * head : 2 * head + 2, :] = queries[4:6, head * HEAD_DIM : (head + 1) * HEAD_DIM]
        fresh = fresh_v[R_DEV + lane].astype(jnp.float32)
        ask_f[16:22, :] = fresh[:, :HEAD_DIM]
        ask_f[32:38, :] = fresh[:, HEAD_DIM:]
        ask_out[lane] = ask_f[...].astype(jnp.bfloat16)

    for copy in kv_load:
        copy.wait()
    for lane in range(LANES):

        def move_part(part, carry, lane=lane):
            where = pl.ds(pl.multiple_of(part * TAIL, TAIL), TAIL)
            send[lane, where, :] = kv[own_row[lane], where, :]
            return carry

        lax.fori_loop(0, CACHE // TAIL, move_part, 0)

    pl.semaphore_wait(barrier, greeted)

    def ask_copy(lane):
        return pltpu.make_async_remote_copy(
            src_ref=ask_out.at[lane], dst_ref=ask_in.at[lane],
            send_sem=ask_send.at[lane], recv_sem=ask_recv.at[lane],
            device_id=(lax.rem(me + INSTANCES - DISTANCES[lane], INSTANCES), tp), device_id_type=MESH,
        )

    def head_copy(lane):
        return pltpu.make_async_remote_copy(
            src_ref=head_out.at[lane], dst_ref=head_in.at[lane],
            send_sem=head_send.at[lane], recv_sem=head_recv.at[lane],
            device_id=(lax.rem(me + DISTANCES[lane], INSTANCES), tp), device_id_type=MESH,
        )

    def bulk_copy(lane, first, rows):
        where = pl.ds(first, rows)
        return pltpu.make_async_remote_copy(
            src_ref=send.at[lane, where], dst_ref=cache_ref.at[lane, where],
            send_sem=bulk_send.at[lane, first // CHUNK], recv_sem=bulk_recv.at[lane],
            device_id=(lax.rem(me + DISTANCES[lane], INSTANCES), tp), device_id_type=MESH,
        )

    def first_leg(lane, source, middle, flip, row):
        slot = RELAY_SLOTS[middle, lane, source, row]
        return pltpu.make_async_remote_copy(
            src_ref=send.at[lane, pl.ds(row, CHUNK)], dst_ref=relay.at[pl.ds(slot * CHUNK, CHUNK)],
            send_sem=bulk_send.at[lane, row // CHUNK], recv_sem=relay_recv.at[slot],
            device_id=((1 - half if flip else half) * 16 + middle, tp), device_id_type=MESH,
        )

    def second_leg(slot, row, lane, source, flip):
        origin = (1 - half if flip else half) * 16 + source
        return pltpu.make_async_remote_copy(
            src_ref=relay.at[pl.ds(slot * CHUNK, CHUNK)], dst_ref=cache_ref.at[lane, pl.ds(row, CHUNK)],
            send_sem=relay_send.at[slot], recv_sem=bulk_recv.at[lane],
            device_id=(lax.rem(origin + DISTANCES[lane], INSTANCES), tp), device_id_type=MESH,
        )

    def landed(slot):
        piece = relay.at[pl.ds(slot * CHUNK, CHUNK)]
        return pltpu.make_async_remote_copy(
            src_ref=piece, dst_ref=piece, send_sem=relay_send.at[slot], recv_sem=relay_recv.at[slot],
            device_id=(lax.rem(me + 1, INSTANCES), tp), device_id_type=MESH,
        )

    def start_lane(lane, chunk):
        direct = None
        for relayed, source, middle, flip, first, last in RELAYS:
            if relayed == lane and first <= chunk < last:

                @pl.when(place == source)
                def _():
                    first_leg(lane, source, middle, flip, chunk * CHUNK).start()

                here = place != source
                direct = here if direct is None else direct & here
        if direct is None:
            bulk_copy(lane, chunk * CHUNK, CHUNK).start()
        else:

            @pl.when(direct)
            def _():
                bulk_copy(lane, chunk * CHUNK, CHUNK).start()

    def forward(chunk):
        for middle, pieces in RELAY_PLAN.items():
            due = [slot for slot in range(len(pieces)) if pieces[slot][0] == chunk * CHUNK]
            if due:

                @pl.when(place == middle)
                def _():
                    for slot in due:
                        landed(slot).wait_recv()
                        second_leg(slot, *pieces[slot]).start()

    def migrate(first, last):
        for step in range(first, last):
            if step < CHUNKS:
                for lane in range(LANES):
                    if step >= DEPTH:
                        bulk_copy(lane, (step - DEPTH) * CHUNK, CHUNK).wait_send()
                    start_lane(lane, step)
            if step >= LAG:
                forward(step - LAG)

    for lane in range(LANES):
        ask_copy(lane).start()
    migrate(0, DEPTH)
    proj_load.start()

    position = lax.broadcasted_iota(jnp.int32, (TAIL, 1), 0) + (CACHE - TAIL)
    for lane in range(LANES):
        ask_copy(lane).wait_recv()
        fresh_key = ask_in[lane, 16:32, :].astype(jnp.float32)
        fresh_value = ask_in[lane, 32:48, :].astype(jnp.float32)
        length = own_length[lane]
        decodes = own_done[lane] < 2
        old = send[lane, CACHE - TAIL : CACHE, :].astype(jnp.float32)
        for part, fresh in ((0, fresh_key), (1, fresh_value)):
            columns = slice(part * HEAD_DIM, (part + 1) * HEAD_DIM)
            new = jnp.where(position < length, old[:, columns], 0.0)
            new = jnp.where((position == length) & decodes, fresh[4:5, :], new)
            new = jnp.where((position == length + 1) & decodes, fresh[5:6, :], new)
            send[lane, CACHE - TAIL : CACHE, columns] = new.astype(jnp.bfloat16)

    for lane in range(LANES):
        scores = dot_t(ask_in[lane, 0:16, :], send[lane, :, :HEAD_DIM]) * SCALE
        key_at = lax.broadcasted_iota(jnp.int32, scores.shape, 1)
        step = lax.broadcasted_iota(jnp.int32, scores.shape, 0) & 1
        scores = jnp.where(key_at <= own_length[lane] + step, scores, MASKED)
        mixed = jnp.dot(softmax_rows(scores), send[lane, :, HEAD_DIM:], preferred_element_type=jnp.float32)
        head_out[lane] = mixed.astype(jnp.bfloat16)
        head_copy(lane).start()
        migrate(*PACE[lane])

    fresh_f[...] = jnp.zeros_like(fresh_f)
    for row in range(R_DEV):
        fresh_f[0:STEPS, :] = fresh_v[row].astype(jnp.float32)
        kv[row, CACHE : CACHE + PAD_KEYS, :] = fresh_f[...].astype(jnp.bfloat16)

    q_f[...] = jnp.zeros_like(q_f)

    def home(index):
        row = stay[index]
        length = lengths_ref[me * R_DEV + row]
        queries = q_v[row].astype(jnp.float32)
        for head in range(GROUP):
            q_f[8 * head : 8 * head + STEPS, :] = queries[:, head * HEAD_DIM : (head + 1) * HEAD_DIM]
        scores = dot_t(q_f[...].astype(jnp.bfloat16), kv[row, :, :HEAD_DIM]) * SCALE
        key_at = lax.broadcasted_iota(jnp.int32, scores.shape, 1)
        step = lax.broadcasted_iota(jnp.int32, scores.shape, 0) & 7
        seen = (key_at < length) | ((key_at >= CACHE) & (key_at - CACHE <= step))
        scores = jnp.where(seen, scores, MASKED)
        mixed = jnp.dot(softmax_rows(scores), kv[row, :, HEAD_DIM:], preferred_element_type=jnp.float32)
        for head in range(GROUP):
            heads[index, 0:STEPS, head * HEAD_DIM : (head + 1) * HEAD_DIM] = mixed[8 * head : 8 * head + STEPS, :]

    for index in range(R_DEV - LANES):
        home(index)
        migrate(*PACE[4 + index])

    migrate(*PACE[8])
    for lane in range(LANES):
        head_copy(lane).wait_recv()
        arrived = head_in[lane].astype(jnp.float32)
        for head in range(GROUP):
            heads[lane, STEPS : STEPS + 2, head * HEAD_DIM : (head + 1) * HEAD_DIM] = arrived[2 * head : 2 * head + 2, :]

    proj_load.wait()
    rows = heads[...].reshape(R_DEV * LANES, GROUP * HEAD_DIM).astype(jnp.bfloat16)

    def pair_copy(hop):
        return pltpu.make_async_remote_copy(
            src_ref=pair_out.at[hop], dst_ref=pair_in.at[hop],
            send_sem=pair_send.at[hop], recv_sem=pair_recv.at[hop],
            device_id=(me, sibling), device_id_type=MESH,
        )

    def part_copy(hop):
        return pltpu.make_async_remote_copy(
            src_ref=part_out.at[hop], dst_ref=part_in.at[hop],
            send_sem=part_send.at[hop], recv_sem=part_recv.at[hop],
            device_id=(me, lax.rem(tp + 2 * hop, TP)), device_id_type=MESH,
        )

    def project(peer):
        columns = pl.ds(pl.multiple_of(peer * COLS, COLS), COLS)
        return jnp.dot(rows, proj[:, columns], preferred_element_type=jnp.float32)

    for index, hop in enumerate(HOPS):
        pair_out[hop] = project(lax.rem(sibling + 2 * hop, TP))
        pair_copy(hop).start()
        migrate(*PACE[9 + index])
    total = None
    for index, hop in enumerate(HOPS):
        mine = project(lax.rem(tp + 2 * hop, TP))
        pair_copy(hop).wait_recv()
        mine = mine + pair_in[hop]
        if hop:
            part_out[hop] = mine.astype(jnp.bfloat16)
            part_copy(hop).start()
        else:
            total = mine
        migrate(*PACE[13 + index])

    migrate(*PACE[17])
    for hop in HOPS[:-1]:
        part_copy(hop).wait_recv()
        total = total + part_in[hop].astype(jnp.float32)
    result[...] = total.reshape(LANES, R_DEV, COLS)

    for row in range(R_DEV):
        found = result[jnp.minimum(stay_place[row], R_DEV - LANES - 1)]
        att_ref[row] = jnp.where(staying[row] == 1, found[0:STEPS, :], 0.0).astype(jnp.bfloat16)
    for lane in range(LANES):
        found = jnp.concatenate([jnp.zeros((4, COLS), jnp.float32), result[lane, STEPS : STEPS + 2, :]], axis=0)
        att_ref[R_DEV + lane] = jnp.where(arrival_done[lane] < 2, found, 0.0).astype(jnp.bfloat16)

    migrate(PACE[17][1], CHUNKS + LAG)

    for lane in range(LANES):
        ask_copy(lane).wait_send()
        head_copy(lane).wait_send()
        for chunk in range(CHUNKS - DEPTH, CHUNKS):
            bulk_copy(lane, chunk * CHUNK, CHUNK).wait_send()
    for hop in HOPS:
        pair_copy(hop).wait_send()
        if hop:
            part_copy(hop).wait_send()

    for middle, pieces in RELAY_PLAN.items():

        @pl.when(place == middle)
        def _():
            for slot, piece in enumerate(pieces):
                second_leg(slot, *piece).wait_send()

    for lane in range(LANES):
        bulk_copy(lane, 0, CACHE).wait_recv()


def write_out(att_ref, cache_ref, att_out, cache_out, sem):
    copies = [pltpu.make_async_copy(cache_ref.at[lane], cache_out.at[lane], sem.at[lane]) for lane in range(LANES)]
    copies.append(pltpu.make_async_copy(att_ref, att_out, sem.at[LANES]))
    for copy in copies:
        copy.start()
    for copy in copies:
        copy.wait()


def local(kv_cache, queries, fresh_kv, out_proj, moving, destination, round_pages, lengths):
    bf16, f32 = jnp.bfloat16, jnp.float32
    row_width = kv_cache.shape[2]
    dma = pltpu.SemaphoreType.DMA
    hbm = pl.BlockSpec(memory_space=pltpu.HBM)
    vmem = pl.BlockSpec(memory_space=pltpu.VMEM)
    slots = R_DEV + LANES
    attended, arrived = pl.pallas_call(
        kernel,
        out_shape=(
            pltpu.VMEM((slots, STEPS, COLS), bf16),
            pltpu.VMEM((LANES, CACHE, row_width), bf16),
        ),
        in_specs=[hbm] * 8,
        out_specs=(vmem, vmem),
        scratch_shapes=[
            pltpu.VMEM((R_DEV, CACHE + PAD_KEYS, row_width), bf16),
            pltpu.VMEM((LANES, CACHE, row_width), bf16),
            pltpu.VMEM((RELAY_PIECES * CHUNK, row_width), bf16),
            pltpu.VMEM(out_proj.shape, bf16),
            pltpu.VMEM(queries.shape, bf16),
            pltpu.VMEM(fresh_kv.shape, bf16),
            pltpu.VMEM((1, moving.shape[0]), jnp.int32),
            pltpu.VMEM((1, moving.shape[0]), jnp.int32),
            pltpu.SMEM((round_pages.shape[1], round_pages.shape[0]), jnp.int32),
            pltpu.SMEM(lengths.shape, jnp.int32),
            pltpu.VMEM((LANES, 48, HEAD_DIM), bf16),
            pltpu.VMEM((LANES, 48, HEAD_DIM), bf16),
            pltpu.VMEM((LANES, 16, HEAD_DIM), bf16),
            pltpu.VMEM((LANES, 16, HEAD_DIM), bf16),
            pltpu.VMEM((8 * GROUP, HEAD_DIM), f32),
            pltpu.VMEM((PAD_KEYS, row_width), f32),
            pltpu.VMEM((48, HEAD_DIM), f32),
            pltpu.VMEM((LANES, R_DEV, GROUP * HEAD_DIM), f32),
            pltpu.VMEM((TP // 2, LANES * R_DEV, COLS), f32),
            pltpu.VMEM((TP // 2, LANES * R_DEV, COLS), f32),
            pltpu.VMEM((TP // 2, LANES * R_DEV, COLS), bf16),
            pltpu.VMEM((TP // 2, LANES * R_DEV, COLS), bf16),
            pltpu.VMEM((LANES, R_DEV, COLS), f32),
            pltpu.SMEM((R_DEV - LANES,), jnp.int32),
            dma((R_DEV,)),
            dma((7,)),
            dma((LANES, CHUNKS)),
            dma((LANES,)),
            dma((RELAY_PIECES,)),
            dma((RELAY_PIECES,)),
            dma((LANES,)),
            dma((LANES,)),
            dma((LANES,)),
            dma((LANES,)),
            dma((TP // 2,)),
            dma((TP // 2,)),
            dma((TP // 2,)),
            dma((TP // 2,)),
        ],
        compiler_params=pltpu.CompilerParams(
            collective_id=0, has_side_effects=True, vmem_limit_bytes=40 * 2**20
        ),
    )(
        *(
            pltpu.with_memory_space_constraint(operand, pltpu.HBM)
            for operand in (
                moving.reshape(1, -1), destination.reshape(1, -1), round_pages.T, lengths,
                kv_cache, queries, fresh_kv, out_proj,
            )
        )
    )
    return pl.pallas_call(
        write_out,
        out_shape=(
            pltpu.HBM((slots, STEPS, COLS), bf16),
            pltpu.HBM((LANES, CACHE, row_width), bf16),
        ),
        in_specs=[vmem, vmem],
        out_specs=(hbm, hbm),
        scratch_shapes=[dma((LANES + 1,))],
        compiler_params=pltpu.CompilerParams(vmem_limit_bytes=16 * 2**20),
    )(pltpu.with_memory_space_constraint(attended, pltpu.VMEM), pltpu.with_memory_space_constraint(arrived, pltpu.VMEM))


def solution(mesh):
    in_specs = (
        P("inst", None, "tp"),
        P("inst", None, "tp"),
        P("inst", None, "tp"),
        P("tp", None),
        P(),
        P(),
        P(),
        P(),
    )
    out_specs = (P("inst", None, "tp"), P("inst", None, "tp"))
    return jax.shard_map(local, mesh=mesh, in_specs=in_specs, out_specs=out_specs, check_vma=False)
```

```python
import functools

import jax
import jax.numpy as jnp
from jax import lax
from jax.experimental import pallas as pl
from jax.experimental.pallas import tpu as pltpu
from jax.sharding import PartitionSpec as P

MESH = pl.DeviceIdType.MESH
HEAD_DIM = 128
R_DEV = 8
LANES = 4
DISTANCES = (1, 2, 8, 16)
INSTANCES = 32
TP = 8
CACHE = 2048
PAD_KEYS = 128
STEPS = 6
GROUP = 8
COLS = 512
CHUNK = 128
CHUNKS = CACHE // CHUNK
TAIL = 256
DEPTH = 3
FREE = 11
DEPTH_LATE = 6
LAG = 6
HOPS = (2, 1, 3, 0)
PACE = ((3, 3), (3, 4), (4, 4), (4, 5), (5, 6), (6, 6), (6, 7), (7, 8), (8, 8), (8, 8), (8, 9), (9, 9), (9, 9), (9, 10), (10, 10), (10, 10), (10, 11), (11, 16))
MASKED = -1e30
SCALE = HEAD_DIM**-0.5

RELAYS = (
    (0, 7, 11, 0, 0, 4),
    (0, 15, 0, 0, 0, 4),
    (0, 15, 3, 0, 4, 8),
    (1, 0, 3, 0, 0, 4),
    (1, 2, 5, 0, 0, 4),
    (1, 2, 7, 0, 4, 8),
    (1, 4, 7, 0, 0, 4),
    (1, 6, 9, 0, 0, 4),
    (1, 8, 11, 0, 0, 4),
    (1, 10, 14, 0, 0, 4),
    (1, 10, 15, 0, 4, 8),
    (1, 12, 15, 0, 0, 4),
    (1, 14, 1, 0, 0, 8),
    (1, 15, 1, 0, 0, 4),
    (1, 15, 2, 0, 4, 12),
    (2, 0, 12, 0, 0, 12),
    (2, 1, 13, 0, 0, 8),
    (2, 8, 4, 0, 0, 12),
    (2, 9, 5, 0, 0, 4),
    (2, 10, 2, 0, 0, 4),
    (2, 11, 7, 0, 0, 4),
    (2, 12, 8, 0, 0, 4),
    (2, 13, 5, 0, 0, 4),
    (2, 14, 6, 0, 0, 12),
    (2, 15, 3, 0, 0, 8),
    (2, 15, 7, 0, 8, 16),
)


def relay_plan():
    plan, slots = {}, {}
    for lane, source, middle, flip, first, last in RELAYS:
        for chunk in range(first, last):
            plan.setdefault(middle, []).append((chunk * CHUNK, lane, source, flip))
    for middle in plan:
        plan[middle].sort()
        for slot, (row, lane, source, flip) in enumerate(plan[middle]):
            slots[middle, lane, source, row] = slot
    base = {(d, 0) for d in DISTANCES} | {(INSTANCES - d, 0) for d in DISTANCES}
    pairs = []

    def meet(first, second, flip):
        shift_a = (second + 16 * flip - first) % INSTANCES
        shift_b = (second - first - 16 * flip) % INSTANCES
        known = all((shift, 0) in base for shift in (shift_a, shift_b))
        entry, back = (first, second, flip), (second, first, flip)
        if not known and entry not in pairs and back not in pairs:
            pairs.append(entry)

    for lane, source, middle, flip, first, last in RELAYS:
        meet(source, middle, flip)
        final = source + DISTANCES[lane]
        meet(middle, final % 16, (flip + final // 16) % 2)
    return plan, slots, tuple(pairs)


RELAY_PLAN, RELAY_SLOTS, EXTRA_PAIRS = relay_plan()
RELAY_PIECES = max([len(pieces) for pieces in RELAY_PLAN.values()], default=1)


def softmax_rows(scores):
    top = jnp.max(scores, axis=-1, keepdims=True)
    grown = jnp.exp(scores - top)
    total = jnp.sum(grown, axis=-1, keepdims=True)
    return (grown * (1.0 / total)).astype(jnp.bfloat16)


def dot_t(a, b):
    return lax.dot_general(a, b, (((1,), (1,)), ((), ())), preferred_element_type=jnp.float32)


def kernel(
    moving_hbm, destination_hbm, pages_hbm, lengths_hbm,
    kv_hbm, q_hbm, fresh_hbm, proj_hbm,
    att_ref, cache_ref,
    kv, send, relay, proj, q_v, fresh_v,
    moving_ref, destination_ref, pages_ref, lengths_ref,
    ask_out, ask_in, head_out, head_in, q_f, fresh_f, ask_f, heads, pair_out, pair_in, part_out, part_in, result, stay,
    kv_sem, load_sem, bulk_send, bulk_recv, relay_recv, relay_send,
    ask_send, ask_recv, head_send, head_recv, pair_send, pair_recv, part_send, part_recv,
):
    me = lax.axis_index("inst")
    tp = lax.axis_index("tp")
    half = me // 16
    place = me % 16

    plan_loads = [
        pltpu.make_async_copy(moving_hbm, moving_ref, load_sem.at[3]),
        pltpu.make_async_copy(destination_hbm, destination_ref, load_sem.at[4]),
        pltpu.make_async_copy(pages_hbm, pages_ref, load_sem.at[5]),
        pltpu.make_async_copy(lengths_hbm, lengths_ref, load_sem.at[6]),
    ]
    small_loads = [
        pltpu.make_async_copy(q_hbm, q_v, load_sem.at[0]),
        pltpu.make_async_copy(fresh_hbm, fresh_v, load_sem.at[1]),
    ]
    kv_load = [
        pltpu.make_async_copy(kv_hbm.at[row], kv.at[row, pl.ds(0, CACHE)], kv_sem.at[row])
        for row in range(R_DEV)
    ]
    proj_load = pltpu.make_async_copy(proj_hbm, proj, load_sem.at[2])
    for copy in plan_loads + small_loads + kv_load:
        copy.start()

    barrier = pltpu.get_barrier_semaphore()

    def greet(inst, peer):
        pl.semaphore_signal(barrier, inc=1, device_id=(inst, peer), device_id_type=MESH)

    for distance in (1, 2, 8, 16, 24, 30, 31):
        greet(lax.rem(me + distance, INSTANCES), tp)
    core = tp % 2
    sibling = tp + 1 - 2 * core
    greet(me, sibling)
    for hop in range(1, TP // 2):
        greet(me, lax.rem(tp + 2 * hop, TP))
    greeted = jnp.int32(7 + TP // 2)
    for first, second, flip in EXTRA_PAIRS:
        other_half = (1 - half if flip else half) * 16

        @pl.when(place == first)
        def _():
            greet(other_half + second, tp)

        @pl.when(place == second)
        def _():
            greet(other_half + first, tp)

        greeted = greeted + jnp.where((place == first) | (place == second), 1, 0)

    for copy in plan_loads:
        copy.wait()
    moving = moving_ref[...]
    destination = destination_ref[...]
    source = moving >> 3
    distance_all = (destination - source) & (INSTANCES - 1)
    code = lax.broadcasted_iota(jnp.int32, moving.shape, 1) * R_DEV + (moving & (R_DEV - 1))
    own_row, own_length, own_done, arrival_done = [], [], [], []

    def done_round(m):
        return jnp.where(pages_ref[2, m] > 0, 2, jnp.where(pages_ref[1, m] > 0, 1, 0))

    for lane in range(LANES):
        on_lane = distance_all == DISTANCES[lane]
        own = jnp.sum(jnp.where(on_lane & (source == me), code, 0))
        arriving = jnp.sum(jnp.where(on_lane & (destination == me), code, 0))
        row = own & (R_DEV - 1)
        own_row.append(row)
        own_length.append(lengths_ref[me * R_DEV + row])
        own_done.append(done_round(own >> 3))
        arrival_done.append(done_round(arriving >> 3))
    staying, stay_place = [], []
    count = jnp.int32(0)
    for row in range(R_DEV):
        gone = own_row[0] == row
        for lane in range(1, LANES):
            gone = gone | (own_row[lane] == row)
        stays = jnp.where(gone, 0, 1)
        staying.append(stays)
        stay_place.append(count)
        count = count + stays
    for index in range(R_DEV - LANES):
        chosen = jnp.int32(0)
        for row in range(R_DEV):
            chosen = jnp.where((staying[row] == 1) & (stay_place[row] == index), row, chosen)
        stay[index] = chosen

    for copy in small_loads:
        copy.wait()
    ask_f[...] = jnp.zeros_like(ask_f)
    for lane in range(LANES):
        queries = q_v[R_DEV + lane].astype(jnp.float32)
        for head in range(GROUP):
            ask_f[2 * head : 2 * head + 2, :] = queries[4:6, head * HEAD_DIM : (head + 1) * HEAD_DIM]
        fresh = fresh_v[R_DEV + lane].astype(jnp.float32)
        ask_f[16:22, :] = fresh[:, :HEAD_DIM]
        ask_f[32:38, :] = fresh[:, HEAD_DIM:]
        ask_out[lane] = ask_f[...].astype(jnp.bfloat16)

    for copy in kv_load:
        copy.wait()
    for lane in range(LANES):

        def move_part(part, carry, lane=lane):
            where = pl.ds(pl.multiple_of(part * TAIL, TAIL), TAIL)
            send[lane, where, :] = kv[own_row[lane], where, :]
            return carry

        lax.fori_loop(0, CACHE // TAIL, move_part, 0)

    pl.semaphore_wait(barrier, greeted)

    def ask_copy(lane):
        return pltpu.make_async_remote_copy(
            src_ref=ask_out.at[lane], dst_ref=ask_in.at[lane],
            send_sem=ask_send.at[lane], recv_sem=ask_recv.at[lane],
            device_id=(lax.rem(me + INSTANCES - DISTANCES[lane], INSTANCES), tp), device_id_type=MESH,
        )

    def head_copy(lane):
        return pltpu.make_async_remote_copy(
            src_ref=head_out.at[lane], dst_ref=head_in.at[lane],
            send_sem=head_send.at[lane], recv_sem=head_recv.at[lane],
            device_id=(lax.rem(me + DISTANCES[lane], INSTANCES), tp), device_id_type=MESH,
        )

    def bulk_copy(lane, first, rows):
        where = pl.ds(first, rows)
        return pltpu.make_async_remote_copy(
            src_ref=send.at[lane, where], dst_ref=cache_ref.at[lane, where],
            send_sem=bulk_send.at[lane, first // CHUNK], recv_sem=bulk_recv.at[lane],
            device_id=(lax.rem(me + DISTANCES[lane], INSTANCES), tp), device_id_type=MESH,
        )

    def first_leg(lane, source, middle, flip, row):
        slot = RELAY_SLOTS[middle, lane, source, row]
        return pltpu.make_async_remote_copy(
            src_ref=send.at[lane, pl.ds(row, CHUNK)], dst_ref=relay.at[pl.ds(slot * CHUNK, CHUNK)],
            send_sem=bulk_send.at[lane, row // CHUNK], recv_sem=relay_recv.at[slot],
            device_id=((1 - half if flip else half) * 16 + middle, tp), device_id_type=MESH,
        )

    def second_leg(slot, row, lane, source, flip):
        origin = (1 - half if flip else half) * 16 + source
        return pltpu.make_async_remote_copy(
            src_ref=relay.at[pl.ds(slot * CHUNK, CHUNK)], dst_ref=cache_ref.at[lane, pl.ds(row, CHUNK)],
            send_sem=relay_send.at[slot], recv_sem=bulk_recv.at[lane],
            device_id=(lax.rem(origin + DISTANCES[lane], INSTANCES), tp), device_id_type=MESH,
        )

    def landed(slot):
        piece = relay.at[pl.ds(slot * CHUNK, CHUNK)]
        return pltpu.make_async_remote_copy(
            src_ref=piece, dst_ref=piece, send_sem=relay_send.at[slot], recv_sem=relay_recv.at[slot],
            device_id=(lax.rem(me + 1, INSTANCES), tp), device_id_type=MESH,
        )

    def start_lane(lane, chunk):
        direct = None
        for relayed, source, middle, flip, first, last in RELAYS:
            if relayed == lane and first <= chunk < last:

                @pl.when(place == source)
                def _():
                    first_leg(lane, source, middle, flip, chunk * CHUNK).start()

                here = place != source
                direct = here if direct is None else direct & here
        if direct is None:
            bulk_copy(lane, chunk * CHUNK, CHUNK).start()
        else:

            @pl.when(direct)
            def _():
                bulk_copy(lane, chunk * CHUNK, CHUNK).start()

    def forward(chunk):
        for middle, pieces in RELAY_PLAN.items():
            due = [slot for slot in range(len(pieces)) if pieces[slot][0] == chunk * CHUNK]
            if due:

                @pl.when(place == middle)
                def _():
                    for slot in due:
                        landed(slot).wait_recv()
                        second_leg(slot, *pieces[slot]).start()

    def gone(step):
        return max(0, min(step, FREE) - DEPTH + 1, step - DEPTH_LATE + 1)

    def migrate(first, last):
        for step in range(first, last):
            if step < CHUNKS:
                for lane in range(LANES):
                    for chunk in range(gone(step - 1), gone(step)):
                        bulk_copy(lane, chunk * CHUNK, CHUNK).wait_send()
                    start_lane(lane, step)
            if step >= LAG:
                forward(step - LAG)

    for lane in range(LANES):
        ask_copy(lane).start()
    migrate(0, DEPTH)
    proj_load.start()

    position = lax.broadcasted_iota(jnp.int32, (TAIL, 1), 0) + (CACHE - TAIL)
    for lane in range(LANES):
        ask_copy(lane).wait_recv()
        fresh_key = ask_in[lane, 16:32, :].astype(jnp.float32)
        fresh_value = ask_in[lane, 32:48, :].astype(jnp.float32)
        length = own_length[lane]
        decodes = own_done[lane] < 2
        old = send[lane, CACHE - TAIL : CACHE, :].astype(jnp.float32)
        for part, fresh in ((0, fresh_key), (1, fresh_value)):
            columns = slice(part * HEAD_DIM, (part + 1) * HEAD_DIM)
            new = jnp.where(position < length, old[:, columns], 0.0)
            new = jnp.where((position == length) & decodes, fresh[4:5, :], new)
            new = jnp.where((position == length + 1) & decodes, fresh[5:6, :], new)
            send[lane, CACHE - TAIL : CACHE, columns] = new.astype(jnp.bfloat16)

    for lane in range(LANES):
        scores = dot_t(ask_in[lane, 0:16, :], send[lane, :, :HEAD_DIM]) * SCALE
        key_at = lax.broadcasted_iota(jnp.int32, scores.shape, 1)
        step = lax.broadcasted_iota(jnp.int32, scores.shape, 0) & 1
        scores = jnp.where(key_at <= own_length[lane] + step, scores, MASKED)
        mixed = jnp.dot(softmax_rows(scores), send[lane, :, HEAD_DIM:], preferred_element_type=jnp.float32)
        head_out[lane] = mixed.astype(jnp.bfloat16)
        head_copy(lane).start()
        migrate(*PACE[lane])

    fresh_f[...] = jnp.zeros_like(fresh_f)
    for row in range(R_DEV):
        fresh_f[0:STEPS, :] = fresh_v[row].astype(jnp.float32)
        kv[row, CACHE : CACHE + PAD_KEYS, :] = fresh_f[...].astype(jnp.bfloat16)

    q_f[...] = jnp.zeros_like(q_f)

    def home(index):
        row = stay[index]
        length = lengths_ref[me * R_DEV + row]
        queries = q_v[row].astype(jnp.float32)
        for head in range(GROUP):
            q_f[8 * head : 8 * head + STEPS, :] = queries[:, head * HEAD_DIM : (head + 1) * HEAD_DIM]
        scores = dot_t(q_f[...].astype(jnp.bfloat16), kv[row, :, :HEAD_DIM]) * SCALE
        key_at = lax.broadcasted_iota(jnp.int32, scores.shape, 1)
        step = lax.broadcasted_iota(jnp.int32, scores.shape, 0) & 7
        seen = (key_at < length) | ((key_at >= CACHE) & (key_at - CACHE <= step))
        scores = jnp.where(seen, scores, MASKED)
        mixed = jnp.dot(softmax_rows(scores), kv[row, :, HEAD_DIM:], preferred_element_type=jnp.float32)
        for head in range(GROUP):
            heads[index, 0:STEPS, head * HEAD_DIM : (head + 1) * HEAD_DIM] = mixed[8 * head : 8 * head + STEPS, :]

    for index in range(R_DEV - LANES):
        home(index)
        migrate(*PACE[4 + index])

    migrate(*PACE[8])
    for lane in range(LANES):
        head_copy(lane).wait_recv()
        arrived = head_in[lane].astype(jnp.float32)
        for head in range(GROUP):
            heads[lane, STEPS : STEPS + 2, head * HEAD_DIM : (head + 1) * HEAD_DIM] = arrived[2 * head : 2 * head + 2, :]

    proj_load.wait()
    rows = heads[...].reshape(R_DEV * LANES, GROUP * HEAD_DIM).astype(jnp.bfloat16)

    def pair_copy(hop):
        return pltpu.make_async_remote_copy(
            src_ref=pair_out.at[hop], dst_ref=pair_in.at[hop],
            send_sem=pair_send.at[hop], recv_sem=pair_recv.at[hop],
            device_id=(me, sibling), device_id_type=MESH,
        )

    def part_copy(hop):
        return pltpu.make_async_remote_copy(
            src_ref=part_out.at[hop], dst_ref=part_in.at[hop],
            send_sem=part_send.at[hop], recv_sem=part_recv.at[hop],
            device_id=(me, lax.rem(tp + 2 * hop, TP)), device_id_type=MESH,
        )

    def project(peer):
        columns = pl.ds(pl.multiple_of(peer * COLS, COLS), COLS)
        return jnp.dot(rows, proj[:, columns], preferred_element_type=jnp.float32)

    for index, hop in enumerate(HOPS):
        pair_out[hop] = project(lax.rem(sibling + 2 * hop, TP))
        pair_copy(hop).start()
        migrate(*PACE[9 + index])
    total = None
    for index, hop in enumerate(HOPS):
        mine = project(lax.rem(tp + 2 * hop, TP))
        pair_copy(hop).wait_recv()
        mine = mine + pair_in[hop]
        if hop:
            part_out[hop] = mine.astype(jnp.bfloat16)
            part_copy(hop).start()
        else:
            total = mine
        migrate(*PACE[13 + index])

    migrate(*PACE[17])
    for hop in HOPS[:-1]:
        part_copy(hop).wait_recv()
        total = total + part_in[hop].astype(jnp.float32)
    result[...] = total.reshape(LANES, R_DEV, COLS)

    for row in range(R_DEV):
        found = result[jnp.minimum(stay_place[row], R_DEV - LANES - 1)]
        att_ref[row] = jnp.where(staying[row] == 1, found[0:STEPS, :], 0.0).astype(jnp.bfloat16)
    for lane in range(LANES):
        found = jnp.concatenate([jnp.zeros((4, COLS), jnp.float32), result[lane, STEPS : STEPS + 2, :]], axis=0)
        att_ref[R_DEV + lane] = jnp.where(arrival_done[lane] < 2, found, 0.0).astype(jnp.bfloat16)

    migrate(PACE[17][1], CHUNKS + LAG)

    for lane in range(LANES):
        ask_copy(lane).wait_send()
        head_copy(lane).wait_send()
        for chunk in range(gone(CHUNKS - 1), CHUNKS):
            bulk_copy(lane, chunk * CHUNK, CHUNK).wait_send()
    for hop in HOPS:
        pair_copy(hop).wait_send()
        if hop:
            part_copy(hop).wait_send()

    for middle, pieces in RELAY_PLAN.items():

        @pl.when(place == middle)
        def _():
            for slot, piece in enumerate(pieces):
                second_leg(slot, *piece).wait_send()

    for lane in range(LANES):
        bulk_copy(lane, 0, CACHE).wait_recv()


def write_out(att_ref, cache_ref, att_out, cache_out, sem):
    copies = [pltpu.make_async_copy(cache_ref.at[lane], cache_out.at[lane], sem.at[lane]) for lane in range(LANES)]
    copies.append(pltpu.make_async_copy(att_ref, att_out, sem.at[LANES]))
    for copy in copies:
        copy.start()
    for copy in copies:
        copy.wait()


def local(kv_cache, queries, fresh_kv, out_proj, moving, destination, round_pages, lengths):
    bf16, f32 = jnp.bfloat16, jnp.float32
    row_width = kv_cache.shape[2]
    dma = pltpu.SemaphoreType.DMA
    hbm = pl.BlockSpec(memory_space=pltpu.HBM)
    vmem = pl.BlockSpec(memory_space=pltpu.VMEM)
    slots = R_DEV + LANES
    attended, arrived = pl.pallas_call(
        kernel,
        out_shape=(
            pltpu.VMEM((slots, STEPS, COLS), bf16),
            pltpu.VMEM((LANES, CACHE, row_width), bf16),
        ),
        in_specs=[hbm] * 8,
        out_specs=(vmem, vmem),
        scratch_shapes=[
            pltpu.VMEM((R_DEV, CACHE + PAD_KEYS, row_width), bf16),
            pltpu.VMEM((LANES, CACHE, row_width), bf16),
            pltpu.VMEM((RELAY_PIECES * CHUNK, row_width), bf16),
            pltpu.VMEM(out_proj.shape, bf16),
            pltpu.VMEM(queries.shape, bf16),
            pltpu.VMEM(fresh_kv.shape, bf16),
            pltpu.VMEM((1, moving.shape[0]), jnp.int32),
            pltpu.VMEM((1, moving.shape[0]), jnp.int32),
            pltpu.SMEM((round_pages.shape[1], round_pages.shape[0]), jnp.int32),
            pltpu.SMEM(lengths.shape, jnp.int32),
            pltpu.VMEM((LANES, 48, HEAD_DIM), bf16),
            pltpu.VMEM((LANES, 48, HEAD_DIM), bf16),
            pltpu.VMEM((LANES, 16, HEAD_DIM), bf16),
            pltpu.VMEM((LANES, 16, HEAD_DIM), bf16),
            pltpu.VMEM((8 * GROUP, HEAD_DIM), f32),
            pltpu.VMEM((PAD_KEYS, row_width), f32),
            pltpu.VMEM((48, HEAD_DIM), f32),
            pltpu.VMEM((LANES, R_DEV, GROUP * HEAD_DIM), f32),
            pltpu.VMEM((TP // 2, LANES * R_DEV, COLS), f32),
            pltpu.VMEM((TP // 2, LANES * R_DEV, COLS), f32),
            pltpu.VMEM((TP // 2, LANES * R_DEV, COLS), bf16),
            pltpu.VMEM((TP // 2, LANES * R_DEV, COLS), bf16),
            pltpu.VMEM((LANES, R_DEV, COLS), f32),
            pltpu.SMEM((R_DEV - LANES,), jnp.int32),
            dma((R_DEV,)),
            dma((7,)),
            dma((LANES, CHUNKS)),
            dma((LANES,)),
            dma((RELAY_PIECES,)),
            dma((RELAY_PIECES,)),
            dma((LANES,)),
            dma((LANES,)),
            dma((LANES,)),
            dma((LANES,)),
            dma((TP // 2,)),
            dma((TP // 2,)),
            dma((TP // 2,)),
            dma((TP // 2,)),
        ],
        compiler_params=pltpu.CompilerParams(
            collective_id=0, has_side_effects=True, vmem_limit_bytes=40 * 2**20
        ),
    )(
        *(
            pltpu.with_memory_space_constraint(operand, pltpu.HBM)
            for operand in (
                moving.reshape(1, -1), destination.reshape(1, -1), round_pages.T, lengths,
                kv_cache, queries, fresh_kv, out_proj,
            )
        )
    )
    return pl.pallas_call(
        write_out,
        out_shape=(
            pltpu.HBM((slots, STEPS, COLS), bf16),
            pltpu.HBM((LANES, CACHE, row_width), bf16),
        ),
        in_specs=[vmem, vmem],
        out_specs=(hbm, hbm),
        scratch_shapes=[dma((LANES + 1,))],
        compiler_params=pltpu.CompilerParams(vmem_limit_bytes=16 * 2**20),
    )(pltpu.with_memory_space_constraint(attended, pltpu.VMEM), pltpu.with_memory_space_constraint(arrived, pltpu.VMEM))


def solution(mesh):
    in_specs = (
        P("inst", None, "tp"),
        P("inst", None, "tp"),
        P("inst", None, "tp"),
        P("tp", None),
        P(),
        P(),
        P(),
        P(),
    )
    out_specs = (P("inst", None, "tp"), P("inst", None, "tp"))
    return jax.shard_map(local, mesh=mesh, in_specs=in_specs, out_specs=out_specs, check_vma=False)
```
